32 devices in a mesh: zone: 4 (over y, x), block: 8 (over z, core).
Axes of the slice: x: 2, y: 2, z: 4, core: 2. Of those that a mesh axis runs over, the one named last changes fastest.
Arguments:
- start_state: float32 [5, 4, 1024, 512], P(None, 'zone', 'block'), may hold values from -6 to 6
- diffusivity: float32 [4, 1024, 512], P('zone', 'block'), may hold values from 0.02 to 0.2
- donor_map: int32 [4, 4, 1024], P(None, 'zone'), may hold values from 0 to 1023, as said below
- donor_weight: float32 [4, 4, 1024], P(None, 'zone'), may hold values from 0 to 1
- coupling: float32 [5, 5], replicated, may hold values from -0.15 to 0.15
- final_cotangent: float32 [5, 4, 1024, 512], P(None, 'zone', 'block'), may hold values from -6 to 6
- wall_area: float32 [4, 3072], P('zone', 'block'), may hold values from 0.5 to 2
- wall_projection: float32 [3, 5], replicated, may hold values from -2.5 to 2.5
- center_ids: int32 [4, 8, 3072], P('zone', None, 'block'), may hold values from 0 to 8191
- center_dist: float32 [4, 8, 3072], P('zone', None, 'block'), may hold values from 0 to 0.95
Outputs:
- adjoint_start: float32 [5, 4, 1024, 512], P(None, 'zone', 'block')
- shape_gradient: float32 [3, 8192], P(None, ('zone', 'block'))
The draws below stay inside these ranges and needn't reach their ends.
Inputs may be any that keep to these rules, and one draw needn't show every extreme that they name: For each step n and zone z there is an offset t, and donor_map[n, z, a] = (a + t + e) mod 1024 with e in 0 to 4.
All inputs are finite; a program needn't handle non-finite values.
Results may differ from the reference program's by a relative error of at most 0.0003.
Values sent between devices are 32-bit elements; how exact they have to be, the bound alone decides.
No kernel may reach another device: no remote copies, remote signals or barrier semaphores. Data moves between devices by JAX's collectives and lax.ppermute only.
A program may use at most 128 MiB of HBM per device.

```python
import math
import jax
import jax.numpy as jnp
from jax import lax

NV = 5
STEPS = 4
KSUP = 8
NODES = 3
NRAD = 512
NZONE = 4
NA = 1024
WALL = 3072
CP = 8192


def draw_donor_map(key, part):
    first_key, second_key = jax.random.split(jax.random.fold_in(key, 11))
    offset = jax.random.randint(first_key, (STEPS, NZONE, 1), 0, NA)
    jitter = jax.random.randint(second_key, (STEPS, NZONE, NA), 0, 5)
    positions = jnp.arange(NA, dtype=jnp.int32)[None, None, :]
    return ((positions + offset + jitter) % NA).astype(jnp.int32)


def place_ends(result, own_key, low, largest):
    dims = result.shape
    spot = [jax.random.randint(jax.random.fold_in(own_key, axis), (), 0, dims[axis]) for axis in range(len(dims))]
    result = result.at[tuple(spot)].set(low)
    longest = dims.index(max(dims))
    spot[longest] = (spot[longest] + 1) % dims[longest]
    return result.at[tuple(spot)].set(largest)


def block_scale(rng, dims, cuts, least, largest):
    gain, own = 1.0, jax.random.fold_in(rng, 6)
    for dim, parts in cuts:
        steps = jnp.exp(jax.random.uniform(jax.random.fold_in(own, dim), (parts,), jnp.float32, least / len(cuts), largest / len(cuts)))
        gain = gain * jnp.repeat(steps, dims[dim] // parts).reshape([-1 if axis == dim else 1 for axis in range(len(dims))])
    return gain


def scatter_about(key, dims, scale, reach, pieces=(), kind=jnp.bfloat16):
    entries = jax.random.normal(key, dims, jnp.float32) * scale
    if len(pieces) > 0:
        entries = block_scale(key, dims, pieces, -0.22, 0.18) * entries
    return jnp.clip(entries, min=-reach, max=reach).astype(kind)


def setup_inputs(seed: int = 0) -> dict:
    splits = jax.random.split(jax.random.key(seed), 11)
    start_state = scatter_about(splits[0], (NV, NZONE, NA, NRAD), 1.0, 6.0, ((1, 4), (2, 8)), jnp.float32)
    diffusivity = jnp.clip(jnp.exp(math.log(0.2) - 2.3025851 * jax.random.uniform(splits[1], (NZONE, NA, NRAD), jnp.float32) ** block_scale(splits[1], (NZONE, NA, NRAD), ((0, 4), (1, 8)), -0.2, 0.2)), 0.02, 0.2)
    donor_map = draw_donor_map(jax.random.fold_in(splits[10], 71), 0)
    donor_weight = jnp.clip(1.0 * jax.random.uniform(splits[3], (STEPS, NZONE, NA), jnp.float32) ** block_scale(splits[3], (STEPS, NZONE, NA), ((1, 4),), -0.2, 0.2), 0.0, 1.0)
    coupling = jnp.clip(jax.random.uniform(splits[4], (NV, NV), jnp.float32, -0.15, 0.15), -0.15, 0.15)
    final_cotangent = scatter_about(splits[5], (NV, NZONE, NA, NRAD), 1.0, 6.0, ((1, 4), (2, 8)), jnp.float32)
    wall_area = jnp.clip(jnp.exp(math.log(2.0) - 1.3862944 * jax.random.uniform(splits[6], (NZONE, WALL), jnp.float32) ** block_scale(splits[6], (NZONE, WALL), ((0, 4), (1, 8)), -0.2, 0.2)), 0.5, 2.0)
    wall_projection = scatter_about(splits[7], (3, NV), NV ** -0.5, 2.5, (), jnp.float32)
    center_ids = place_ends(jax.random.randint(splits[8], (NZONE, KSUP, WALL), 0, CP), jax.random.fold_in(splits[8], 1), 0, CP - 1).astype(jnp.int32)
    center_dist = jnp.clip(0.95 * jax.random.uniform(splits[9], (NZONE, KSUP, WALL), jnp.float32) ** block_scale(splits[9], (NZONE, KSUP, WALL), ((0, 4), (2, 8)), -0.2, 0.2), 0.0, 0.95)
    return {"start_state": start_state, "diffusivity": diffusivity, "donor_map": donor_map, "donor_weight": donor_weight, "coupling": coupling, "final_cotangent": final_cotangent, "wall_area": wall_area, "wall_projection": wall_projection, "center_ids": center_ids, "center_dist": center_dist}


def advance(field, diffusivity, donor_rows, donor_share, coupling):
    row_total = field.shape[2]
    zone_total = field.shape[1]
    outer_face = field[:, :, :, -1]
    partner_face = outer_face[:, jnp.bitwise_xor(jnp.arange(zone_total, dtype=jnp.int32), 1)]
    second_rows = (donor_rows + 1) % row_total
    donor_first = jnp.take_along_axis(partner_face, donor_rows[None], axis=2)
    donor_second = jnp.take_along_axis(partner_face, second_rows[None], axis=2)
    ghost = donor_share[None] * donor_first + (1.0 - donor_share[None]) * donor_second
    outward = jnp.concatenate([field[..., 1:], ghost[..., None]], axis=-1)
    inward = jnp.concatenate([jnp.zeros_like(field[..., :1]), field[..., :-1]], axis=-1)
    laplace = jnp.roll(field, -1, axis=2) + jnp.roll(field, 1, axis=2) + outward + inward - 4.0 * field
    reaction = jnp.einsum('vw,wzar->vzar', coupling, jnp.tanh(field), precision=lax.Precision.HIGHEST)
    return field + diffusivity[None] * laplace - reaction

def reference(start_state, diffusivity, donor_map, donor_weight, coupling, final_cotangent, wall_area, wall_projection, center_ids, center_dist):
    history = [start_state]
    for time_step in range(STEPS - 1):
        history.append(advance(history[-1], diffusivity, donor_map[time_step], donor_weight[time_step], coupling))
    adjoint = final_cotangent
    wall_product = jnp.zeros(start_state.shape[:3], jnp.float32)
    for time_step in reversed(range(STEPS)):
        wall_product = wall_product + adjoint[..., 0] * history[time_step][..., 0]

        def forward(state, time_step=time_step):
            return advance(state, diffusivity, donor_map[time_step], donor_weight[time_step], coupling)
        _, pullback = jax.vjp(forward, history[time_step])
        adjoint = pullback(adjoint)[0]
    repeated = jnp.repeat(wall_product, NODES, axis=2)
    sensitivity = wall_area[None] * jnp.einsum('cv,vzw->czw', wall_projection, repeated, precision=lax.Precision.HIGHEST)
    kernel = (1.0 - center_dist) ** 4 * (4.0 * center_dist + 1.0)
    weighted = kernel[None] * sensitivity[:, :, None, :]
    gradient = jnp.zeros((3, CP), jnp.float32).at[:, center_ids.reshape(-1)].add(weighted.reshape(3, -1))
    return (adjoint, gradient)
```

```python
import functools

import jax
import jax.numpy as jnp
from jax import lax
from jax.experimental import pallas as pl
from jax.experimental.pallas import tpu as pltpu
from jax.sharding import PartitionSpec as P

CP_DEV = 256
LANES = 128
SUB = 8
STEPS = 4
NV = 5
UCOLS = STEPS + 2
LCOLS = STEPS
HALO = SUB
ROW_K = 2 * STEPS
ROW_U = ROW_K + UCOLS
ROW_L = ROW_U + NV * UCOLS
STRIP = ROW_L + NV * LCOLS
VMEM_LIMIT = 48 * 1024 * 1024


def params(**kw):
    return pltpu.CompilerParams(vmem_limit_bytes=VMEM_LIMIT, **kw)


def pack_kernel(
    u_in, u_out, l_in, l_out, k_in, k_out, u_lo, u_hi, l_lo, l_hi, k_lo, k_hi, dmap, dweight,
    strip, wall, low, high,
):
    rows = u_in.shape[2]
    block = lax.axis_index("block")
    own = pl.ds(pl.multiple_of(block * rows, LANES), rows)
    strip[0:STEPS, :] = dmap[:, 0, own].astype(jnp.float32)
    strip[STEPS : 2 * STEPS, :] = dweight[:, 0, own]
    kt = k_out[0].T
    strip[ROW_K : ROW_K + UCOLS, :] = kt[LANES - UCOLS :]
    wall[ROW_K : ROW_K + UCOLS, :] = k_in[0].T[:UCOLS]
    wall[0:ROW_K, :] = jnp.zeros((ROW_K, rows), jnp.float32)
    for v in range(NV):
        a, b = ROW_U + v * UCOLS, ROW_L + v * LCOLS
        strip[a : a + UCOLS, :] = u_out[v, 0].T[LANES - UCOLS :]
        strip[b : b + LCOLS, :] = l_out[v, 0].T[LANES - LCOLS :]
        wall[a : a + UCOLS, :] = u_in[v, 0].T[:UCOLS]
        wall[b : b + LCOLS, :] = l_in[v, 0].T[:LCOLS]
    for ref, u, l, k in ((low, u_lo, l_lo, k_lo), (high, u_hi, l_hi, k_hi)):
        ref[0:NV] = u[:, 0]
        ref[NV : 2 * NV] = l[:, 0]
        ref[2 * NV] = k[0]


def pack(start_state, final_cotangent, diffusivity, donor_map, donor_weight):
    _, _, rows, radial = start_state.shape
    last_tile, last_rows = radial // LANES - 1, rows // HALO - 1

    def side(tile):
        return pl.BlockSpec((NV, 1, rows, LANES), lambda i: (0, 0, 0, tile))

    def kside(tile):
        return pl.BlockSpec((1, rows, LANES), lambda i: (0, 0, tile))

    def edge(index):
        return pl.BlockSpec((NV, 1, HALO, radial), lambda i: (0, 0, index, 0))

    def kedge(index):
        return pl.BlockSpec((1, HALO, radial), lambda i: (0, index, 0))

    def whole(shape):
        return pl.BlockSpec(shape, lambda i: (0,) * len(shape))

    f32 = jnp.float32
    outs = ((STRIP, rows), (STRIP, rows), (2 * NV + 1, HALO, radial), (2 * NV + 1, HALO, radial))
    u, l, k = start_state, final_cotangent, diffusivity
    return pl.pallas_call(
        pack_kernel,
        grid=(1,),
        in_specs=[
            side(0), side(last_tile), side(0), side(last_tile), kside(0), kside(last_tile),
            edge(0), edge(last_rows), edge(0), edge(last_rows), kedge(0), kedge(last_rows),
            whole(donor_map.shape), whole(donor_weight.shape),
        ],
        out_specs=[whole(s) for s in outs],
        out_shape=[jax.ShapeDtypeStruct(s, f32) for s in outs],
        compiler_params=params(),
        name="pack",
    )(u, u, l, l, k, k, u, u, l, l, k, k, donor_map, donor_weight)


def iota(shape, axis):
    return lax.broadcasted_iota(jnp.int32, shape, axis)


def left(x, by=1):
    return pltpu.roll(x, x.shape[-1] - by, x.ndim - 1)


def right(x, by=1):
    return pltpu.roll(x, by, x.ndim - 1)


def stencil(x, inner, outer):
    sub = iota(x.shape, 0)
    out = pltpu.roll(x, SUB - 1, 0)
    inn = pltpu.roll(x, 1, 0)
    if outer is not None:
        out = jnp.where(sub == SUB - 1, outer, out)
    if inner is not None:
        inn = jnp.where(sub == 0, inner, inn)
    return left(x) + right(x) + out + inn - 4.0 * x


def strip_forward(u, t, kappa, c, inner, outer):
    new = []
    for v in range(NV):
        reaction = sum(c[v, w] * t[w] for w in range(NV))
        lap = stencil(u[v], inner, None if outer is None else outer[v])
        new.append(u[v] + kappa * lap - reaction)
    return new


def strip_backward(lam, t, kappa, c, inner, outer):
    new = []
    for v in range(NV):
        pulled = sum(c[w, v] * lam[w] for w in range(NV))
        lap = stencil(kappa * lam[v], inner, None if outer is None else outer[v])
        new.append(lam[v] + lap - (1.0 - t[v] * t[v]) * pulled)
    return new


def wall_kernel(own, before, after, c, proj, area, ids, dist, out, *, count):
    rows = own.shape[1]

    def rows_of(a, b):
        return jnp.concatenate([before[a:b, :], own[a:b, :], after[a:b, :]], axis=1)

    def first(start, cols):
        piece = rows_of(start, start + cols)
        pad = jnp.zeros((SUB - cols, piece.shape[1]), jnp.float32)
        return jnp.concatenate([piece, pad], axis=0)

    kappa = first(ROW_K, UCOLS)
    u = [first(ROW_U + v * UCOLS, UCOLS) for v in range(NV)]
    lam = [first(ROW_L + v * LCOLS, LCOLS) for v in range(NV)]
    history = []
    for n in range(STEPS):
        t = [jnp.tanh(x) for x in u]
        history.append((u, t))
        if n < STEPS - 1:
            u = strip_forward(u, t, kappa, c, 0.0, None)
    h = [0.0] * NV
    for n in reversed(range(STEPS)):
        u, t = history[n]
        h = [h[v] + (lam[v] * u[v])[0:1, rows : 2 * rows] for v in range(NV)]
        if n > 0:
            lam = strip_backward(lam, t, kappa, c, 0.0, None)
    nodes = area.shape[1]
    per_row = nodes // rows
    s_rows = [sum(proj[i, v] * h[v] for v in range(NV)) for i in range(3)]
    s_rows = jnp.concatenate(s_rows + [jnp.zeros((SUB - 3, rows), jnp.float32)], axis=0)
    spread = (iota((rows, nodes), 1) // per_row == iota((rows, nodes), 0)).astype(jnp.float32)
    s = jnp.dot(s_rows, spread, precision=lax.Precision.HIGHEST, preferred_element_type=jnp.float32)
    s = s * area[...]
    d = dist[0]
    q = 1.0 - d
    q = q * q
    phi = q * q * (4.0 * d + 1.0)
    key = ids[0]
    major, minor = key // LANES, key % LANES
    groups = count // LANES
    total = jnp.zeros((3 * groups, LANES), jnp.float32)
    bf = jnp.bfloat16
    for k in range(d.shape[0]):
        lo = (iota((LANES, nodes), 0) == minor[k : k + 1]).astype(bf)
        hit = iota((groups, nodes), 0) == major[k : k + 1]
        w = s[0:3] * phi[k : k + 1]
        for piece in range(3):
            part = w.astype(bf).astype(jnp.float32)
            w = w - part
            a = jnp.concatenate([jnp.where(hit, part[i : i + 1], 0.0) for i in range(3)], axis=0)
            total += lax.dot_general(
                a.astype(bf), lo, (((1,), (1,)), ((), ())), preferred_element_type=jnp.float32
            )
    out[...] = total


def wall_gradient(own, before, after, coupling, proj, area, ids, dist, count):
    vm = pl.BlockSpec(memory_space=pltpu.VMEM)
    sm = pl.BlockSpec(memory_space=pltpu.SMEM)
    return pl.pallas_call(
        functools.partial(wall_kernel, count=count),
        in_specs=[vm, vm, vm, sm, sm, vm, vm, vm],
        out_specs=vm,
        out_shape=jax.ShapeDtypeStruct((3 * count // LANES, LANES), jnp.float32),
        compiler_params=params(),
        name="wall_gradient",
    )(own, before, after, coupling, proj, area, ids, dist)


def face_kernel(pieces, c, out, face, flip, *, rows):
    block = lax.axis_index("block")
    blocks = pieces.shape[0] // 2
    half = blocks // 2
    total = blocks * rows

    def piece(q, a, b):
        parts = []
        for j in range(blocks):
            rel = block ^ j
            slot = (rel & 1) * blocks + q * half + (rel >> 1)
            parts.append(pieces[slot, a:b, :])
        return jnp.concatenate(parts, axis=1)

    def last(q, end):
        return piece(q, end - SUB, end)

    lane = iota((SUB, total), 1).astype(jnp.float32)
    sub = iota((SUB, total), 0)
    size = float(total)
    shift, taps = [], []
    for q in range(2):
        donors = piece(q, 0, SUB)
        share = jnp.concatenate([donors[STEPS:], donors[STEPS:]], axis=0)
        delta = donors - lane
        delta = jnp.where(delta < 0.0, delta + size, delta)
        rel = delta - delta[:, 0:1] + float(STEPS)
        rel = jnp.where(rel < 0.0, rel + size, rel)
        rel = jnp.where(rel >= size, rel - size, rel)
        least = jnp.min(rel, axis=1, keepdims=True)
        e = rel - least
        t = delta[:, 0:1] - float(STEPS) + least
        t = jnp.where(t < 0.0, t + size, t)
        t = jnp.where(t >= size, t - size, t).astype(jnp.int32)
        shift.append([t[n, 0] for n in range(STEPS)])
        coefs = [
            jnp.where(e == float(i), share, 0.0) + jnp.where(e == float(i - 1), 1.0 - share, 0.0)
            for i in range(6)
        ]
        taps.append([[coefs[i][n : n + 1] for i in range(6)] for n in range(STEPS)])

    kappa = [last(q, ROW_K + UCOLS) for q in range(2)]
    u = [[last(q, ROW_U + (v + 1) * UCOLS) for v in range(NV)] for q in range(2)]
    lam = [[last(q, ROW_L + (v + 1) * LCOLS) for v in range(NV)] for q in range(2)]
    face[...] = jnp.zeros_like(face)

    def gather_faces(q, x):
        for v in range(NV):
            face[q, v : v + 1, :] = x[v][SUB - 1 : SUB, :]
        return face[q]

    def ghost(q, n, f):
        f = pltpu.roll(f, (total - shift[q][n]) % total, 1)
        acc = taps[q][n][0] * f
        for i in range(1, 6):
            f = left(f)
            acc = acc + taps[q][n][i] * f
        return acc

    def back(q, n, f):
        acc = taps[q][n][5] * f
        for i in reversed(range(5)):
            acc = right(acc) + taps[q][n][i] * f
        return pltpu.roll(acc, shift[q][n], 1)

    def rows_apart(g):
        return [jnp.broadcast_to(g[v : v + 1], (SUB, total)) for v in range(NV)]

    offset = (total + HALO - block * rows) % total
    width = 2 * LANES

    def emit(index, g):
        g = pltpu.roll(g, offset, 1)
        flip[index * SUB : (index + 1) * SUB, :] = g[:, :width]

    flip[...] = jnp.zeros_like(flip)
    history = []
    for n in range(STEPS):
        t = [[jnp.tanh(x) for x in u[q]] for q in range(2)]
        history.append(t)
        if n < STEPS - 1:
            faces = [gather_faces(q, u[q]) for q in range(2)]
            g = [ghost(q, n, faces[1 - q]) for q in range(2)]
            emit(n, g[0])
            u = [
                strip_forward(u[q], t[q], kappa[q], c, None, rows_apart(g[q])) for q in range(2)
            ]
    for n in reversed(range(STEPS)):
        t = history[n]
        faces = [gather_faces(q, [kappa[q] * x for x in lam[q]]) for q in range(2)]
        g = [back(1 - q, n, faces[1 - q]) if n > 0 or q == 0 else None for q in range(2)]
        emit(STEPS - 1 + n, g[0])
        if n > 0:
            lam = [
                strip_backward(lam[q], t[q], kappa[q], c, None, rows_apart(g[q]))
                for q in range(2)
            ]
    for j in range(2):
        out[j * LANES : (j + 1) * LANES, :] = flip[:, j * LANES : (j + 1) * LANES].T


def face_terms(pieces, coupling, rows):
    vm = pl.BlockSpec(memory_space=pltpu.VMEM)
    sm = pl.BlockSpec(memory_space=pltpu.SMEM)
    total = pieces.shape[0] // 2 * rows
    return pl.pallas_call(
        functools.partial(face_kernel, rows=rows),
        in_specs=[vm, sm],
        out_specs=vm,
        out_shape=jax.ShapeDtypeStruct((2 * LANES, LANES), jnp.float32),
        scratch_shapes=[
            pltpu.VMEM((2, SUB, total), jnp.float32),
            pltpu.VMEM((LANES, 2 * LANES), jnp.float32),
        ],
        compiler_params=params(),
        name="face_terms",
    )(pieces, coupling)


def field_kernel(
    u_hbm, l_hbm, k_hbm, before, after, terms, c, out,
    ext_u, ext_l, ext_k, kap, states, tanhs, lam, scaled, sems,
):
    rows, radial = u_hbm.shape[2], u_hbm.shape[3]
    chunks = kap.shape[0]
    tiles = radial // LANES
    own = pl.ds(HALO, rows)

    def cut(j):
        return slice(j * LANES, (j + 1) * LANES)

    copies = []
    for j in range(tiles):
        lanes = pl.ds(j * LANES, LANES)
        copies += [
            pltpu.make_async_copy(u_hbm.at[:, 0, :, lanes], ext_u.at[:, j, own], sems.at[0, j]),
            pltpu.make_async_copy(l_hbm.at[:, 0, :, lanes], ext_l.at[:, j, own], sems.at[1, j]),
            pltpu.make_async_copy(k_hbm.at[0, :, lanes], ext_k.at[j, own], sems.at[2, j]),
        ]
    for copy in copies:
        copy.start()
    for ref, at in ((before, 0), (after, HALO + rows)):
        for j in range(tiles):
            ext_u[:, j, at : at + HALO] = ref[0:NV, :, cut(j)]
            ext_l[:, j, at : at + HALO] = ref[NV : 2 * NV, :, cut(j)]
            ext_k[j, at : at + HALO] = ref[2 * NV, :, cut(j)]
    for copy in copies:
        copy.wait()

    def load(i, carry):
        at = pl.ds(i, SUB, stride=chunks)
        for j in range(tiles):
            kappa = ext_k[j, at, :]
            kap[i, :, cut(j)] = kappa
            for v in range(NV):
                states[0, v, i + 1, :, cut(j)] = ext_u[v, j, at, :]
                x = ext_l[v, j, at, :]
                lam[v, i, :, cut(j)] = x
                scaled[0, v, i + 1, :, cut(j)] = kappa * x
        return carry

    lax.fori_loop(0, chunks, load, 0)

    def wrap(ref):
        for v in range(NV):
            ref[v, 0] = pltpu.roll(ref[v, chunks], 1, 0)
            ref[v, chunks + 1] = pltpu.roll(ref[v, 1], SUB - 1, 0)

    wrap(states.at[0])
    wrap(scaled.at[0])
    lane = iota((SUB, LANES), 1)
    is_first, is_last = lane == 0, lane == LANES - 1

    def neighbours(ref, v, i, j, edge, cache):
        def tile(b):
            if (v, b) not in cache:
                x = ref[v, i + 1, :, cut(b)]
                cache[v, b] = (x, pltpu.roll(x, 1, 1), pltpu.roll(x, LANES - 1, 1))
            return cache[v, b]

        x, r, l = tile(j)
        inn = jnp.where(is_first, tile(j - 1)[1] if j > 0 else 0.0, r)
        outv = jnp.where(is_last, tile(j + 1)[2] if j < tiles - 1 else edge, l)
        return ref[v, i, :, cut(j)] + ref[v, i + 2, :, cut(j)] + inn + outv, x

    def edges(i, n):
        e = terms[pl.ds(i, SUB, stride=chunks), :]
        return [pltpu.roll(e, (2 * LANES - 1 - (n * SUB + v)) % LANES, 1) for v in range(NV)]

    def forward(n):
        def body(i, carry):
            edge = edges(i, n)
            cache = {}
            for j in range(tiles):
                kappa = kap[i, :, cut(j)]
                pairs = [neighbours(states.at[n], v, i, j, edge[v], cache) for v in range(NV)]
                t = [jnp.tanh(x) for _, x in pairs]
                for v in range(NV):
                    around, x = pairs[v]
                    tanhs[n, v, i, :, cut(j)] = t[v]
                    reaction = sum(c[v, w] * t[w] for w in range(NV))
                    states[n + 1, v, i + 1, :, cut(j)] = (
                        x + kappa * (around - 4.0 * x) - reaction
                    )
            return carry

        lax.fori_loop(0, chunks, body, 0)
        if n + 1 < STEPS - 1:
            wrap(states.at[n + 1])

    def backward(n, source, target):
        def body(i, carry):
            edge = edges(i, STEPS - 1 + n)
            cache = {}
            for j in range(tiles):
                kappa = kap[i, :, cut(j)]
                pairs = [neighbours(scaled.at[source], v, i, j, edge[v], cache) for v in range(NV)]
                x = [lam[v, i, :, cut(j)] for v in range(NV)]
                for v in range(NV):
                    if n < STEPS - 1:
                        t = tanhs[n, v, i, :, cut(j)]
                    else:
                        t = jnp.tanh(states[n, v, i + 1, :, cut(j)])
                    around, s = pairs[v]
                    pulled = sum(c[w, v] * x[w] for w in range(NV))
                    new = x[v] + (around - 4.0 * s) - (1.0 - t * t) * pulled
                    if n > 0:
                        lam[v, i, :, cut(j)] = new
                        scaled[target, v, i + 1, :, cut(j)] = kappa * new
                    else:
                        ext_l[v, j, pl.ds(i, SUB, stride=chunks), :] = new
            return carry

        lax.fori_loop(0, chunks, body, 0)
        if n > 0:
            wrap(scaled.at[target])

    for n in range(STEPS - 1):
        forward(n)
    source = 0
    for n in reversed(range(STEPS)):
        backward(n, source, 1 - source)
        source = 1 - source
    copies = [
        pltpu.make_async_copy(
            ext_l.at[:, j, own], out.at[:, 0, :, pl.ds(j * LANES, LANES)], sems.at[3, j]
        )
        for j in range(tiles)
    ]
    for copy in copies:
        copy.start()
    for copy in copies:
        copy.wait()


def field(start_state, final_cotangent, diffusivity, before, after, terms, coupling):
    _, _, rows, radial = start_state.shape
    ext = rows + 2 * HALO
    chunks, tiles = ext // SUB, radial // LANES
    vm = pl.BlockSpec(memory_space=pltpu.VMEM)
    hbm = pl.BlockSpec(memory_space=pl.ANY)
    f32 = jnp.float32
    return pl.pallas_call(
        field_kernel,
        in_specs=[hbm, hbm, hbm, vm, vm, vm, pl.BlockSpec(memory_space=pltpu.SMEM)],
        out_specs=hbm,
        out_shape=jax.ShapeDtypeStruct(start_state.shape, f32),
        scratch_shapes=[
            pltpu.VMEM((NV, tiles, ext, LANES), f32),
            pltpu.VMEM((NV, tiles, ext, LANES), f32),
            pltpu.VMEM((tiles, ext, LANES), f32),
            pltpu.VMEM((chunks, SUB, radial), f32),
            pltpu.VMEM((STEPS, NV, chunks + 2, SUB, radial), f32),
            pltpu.VMEM((STEPS - 1, NV, chunks, SUB, radial), f32),
            pltpu.VMEM((NV, chunks, SUB, radial), f32),
            pltpu.VMEM((2, NV, chunks + 2, SUB, radial), f32),
            pltpu.SemaphoreType.DMA((4, tiles)),
        ],
        compiler_params=params(),
        name="field",
    )(start_state, final_cotangent, diffusivity, before, after, terms, coupling)


def ring(x, step):
    size = lax.axis_size("block")
    return lax.ppermute(x, "block", [(i, (i + step) % size) for i in range(size)])


def crossed(x, mask):
    return lax.ppermute(x, "block", [(i, i ^ mask) for i in range(lax.axis_size("block"))])


def swapped(x):
    return lax.ppermute(x, "zone", [(i, i ^ 1) for i in range(lax.axis_size("zone"))])


def gather_pair(strip):
    x = strip[None]
    bit, size = 1, lax.axis_size("block")
    while 2**bit < size:
        wide = 4 if 2 ** (bit + 1) < size else 2
        x = jnp.concatenate([x] + [crossed(x, k << bit) for k in range(1, wide)], axis=0)
        bit += 2 if wide == 4 else 1
    x = jnp.concatenate([x, swapped(x)], axis=0)
    return jnp.concatenate([x, crossed(x, 1)], axis=0)


def local(
    start_state,
    diffusivity,
    donor_map,
    donor_weight,
    coupling,
    final_cotangent,
    wall_area,
    wall_projection,
    center_ids,
    center_dist,
):
    rows = start_state.shape[2]
    devices = lax.axis_size("zone") * lax.axis_size("block")
    strip, wall, low, high = pack(
        start_state, final_cotangent, diffusivity, donor_map, donor_weight
    )
    wall_before, wall_after = ring(wall, 1), ring(wall, -1)
    before, after = ring(high, 1), ring(low, -1)
    pieces = gather_pair(strip)
    points = wall_gradient(
        wall, wall_before, wall_after, coupling, wall_projection, wall_area, center_ids,
        center_dist, CP_DEV * devices,
    )
    groups = CP_DEV // LANES
    points = points.reshape(3, devices, groups, LANES).transpose(1, 0, 2, 3)
    points = lax.all_to_all(points, ("zone", "block"), 0, 0, tiled=True)
    gradient = points.sum(axis=0).reshape(3, CP_DEV)
    terms = face_terms(pieces, coupling, rows)
    adjoint = field(start_state, final_cotangent, diffusivity, before, after, terms, coupling)
    return adjoint, gradient


def solution(mesh):
    return jax.shard_map(
        local,
        mesh=mesh,
        in_specs=(
            P(None, "zone", "block", None),
            P("zone", "block", None),
            P(None, "zone", None),
            P(None, "zone", None),
            P(),
            P(None, "zone", "block", None),
            P("zone", "block"),
            P(),
            P("zone", None, "block"),
            P("zone", None, "block"),
        ),
        out_specs=(P(None, "zone", "block", None), P(None, ("zone", "block"))),
        check_vma=False,
    )
```

```python
import functools

import jax
import jax.numpy as jnp
from jax import lax
from jax.experimental import pallas as pl
from jax.experimental.pallas import tpu as pltpu
from jax.sharding import PartitionSpec as P

CP_DEV = 256
LANES = 128
SUB = 8
STEPS = 4
NV = 5
UCOLS = STEPS + 2
LCOLS = STEPS
HALO = SUB
ROW_K = 2 * STEPS
ROW_U = ROW_K + UCOLS
ROW_L = ROW_U + NV * UCOLS
STRIP = ROW_L + NV * LCOLS
WALL = STRIP - ROW_K
EDGE_L = NV * UCOLS
EDGE_K = EDGE_L + NV * LCOLS
EDGE_W = EDGE_K + UCOLS
WALL_ROWS = 2 * SUB
EDGE = EDGE_W + WALL_ROWS
TAPS = 6
VMEM_LIMIT = 48 * 1024 * 1024


def params(**kw):
    return pltpu.CompilerParams(vmem_limit_bytes=VMEM_LIMIT, **kw)


def pack_kernel(
    u_hbm, l_hbm, k_hbm, map_hbm, weight_hbm, strip, wall, low, high,
    u_side, l_side, k_side, u_edge, l_edge, k_edge, dmap, dweight, sems,
):
    rows, radial = u_hbm.shape[2], u_hbm.shape[3]
    tiles = radial // LANES
    block = lax.axis_index("block")
    own = pl.ds(pl.multiple_of(block * rows, LANES), rows)
    copies = [
        pltpu.make_async_copy(map_hbm.at[:, 0, own], dmap, sems.at[0, 0]),
        pltpu.make_async_copy(weight_hbm.at[:, 0, own], dweight, sems.at[0, 1]),
    ]
    for i, start in enumerate((0, radial - LANES)):
        lanes = pl.ds(start, LANES)
        copies += [
            pltpu.make_async_copy(u_hbm.at[:, 0, :, lanes], u_side.at[i], sems.at[1, i]),
            pltpu.make_async_copy(l_hbm.at[:, 0, :, lanes], l_side.at[i], sems.at[2, i]),
            pltpu.make_async_copy(k_hbm.at[0, :, lanes], k_side.at[i], sems.at[3, i]),
        ]
    for i, start in enumerate((0, rows - SUB)):
        some = pl.ds(start, SUB)
        copies += [
            pltpu.make_async_copy(u_hbm.at[:, 0, some], u_edge.at[i], sems.at[4, i]),
            pltpu.make_async_copy(l_hbm.at[:, 0, some], l_edge.at[i], sems.at[5, i]),
            pltpu.make_async_copy(k_hbm.at[0, some], k_edge.at[i], sems.at[6, i]),
        ]
    for copy in copies:
        copy.start()
    for copy in copies:
        copy.wait()
    strip[0:STEPS, :] = dmap[...].astype(jnp.float32)
    strip[STEPS : 2 * STEPS, :] = dweight[...]
    strip[ROW_K : ROW_K + UCOLS, :] = k_side[1].T[LANES - UCOLS :]
    wall[0:UCOLS, :] = k_side[0].T[:UCOLS]
    for v in range(NV):
        a, b = ROW_U + v * UCOLS, ROW_L + v * LCOLS
        strip[a : a + UCOLS, :] = u_side[1, v].T[LANES - UCOLS :]
        strip[b : b + LCOLS, :] = l_side[1, v].T[LANES - LCOLS :]
        a, b = a - ROW_K, b - ROW_K
        wall[a : a + UCOLS, :] = u_side[0, v].T[:UCOLS]
        wall[b : b + LCOLS, :] = l_side[0, v].T[:LCOLS]
    for i, ref in enumerate((low, high)):
        few = slice(0, UCOLS) if i == 0 else slice(SUB - UCOLS, SUB)
        fewer = slice(0, LCOLS) if i == 0 else slice(SUB - LCOLS, SUB)
        for v in range(NV):
            ref[v * UCOLS : (v + 1) * UCOLS, :] = u_edge[i, v, few, :]
            ref[EDGE_L + v * LCOLS : EDGE_L + (v + 1) * LCOLS, :] = l_edge[i, v, fewer, :]
        ref[EDGE_K:EDGE_W, :] = k_edge[i, few, :]
        for j in range(tiles):
            some = wall[min(j * WALL_ROWS, WALL) : min((j + 1) * WALL_ROWS, WALL), :]
            if some.shape[0] < WALL_ROWS:
                gap = jnp.zeros((WALL_ROWS - some.shape[0], rows), jnp.float32)
                some = jnp.concatenate([some, gap], axis=0) if some.shape[0] else gap
            ref[EDGE_W:EDGE, j * LANES : (j + 1) * LANES] = some


def pack(start_state, final_cotangent, diffusivity, donor_map, donor_weight):
    _, _, rows, radial = start_state.shape
    f32 = jnp.float32
    outs = ((STRIP, rows), (WALL, rows), (EDGE, radial), (EDGE, radial))
    return pl.pallas_call(
        pack_kernel,
        in_specs=[pl.BlockSpec(memory_space=pltpu.HBM)] * 5,
        out_specs=[pl.BlockSpec(memory_space=pltpu.VMEM)] * 4,
        out_shape=[jax.ShapeDtypeStruct(s, f32) for s in outs],
        scratch_shapes=[
            pltpu.VMEM((2, NV, rows, LANES), f32),
            pltpu.VMEM((2, NV, rows, LANES), f32),
            pltpu.VMEM((2, rows, LANES), f32),
            pltpu.VMEM((2, NV, SUB, radial), f32),
            pltpu.VMEM((2, NV, SUB, radial), f32),
            pltpu.VMEM((2, SUB, radial), f32),
            pltpu.VMEM((STEPS, rows), jnp.int32),
            pltpu.VMEM((STEPS, rows), f32),
            pltpu.SemaphoreType.DMA((7, 2)),
        ],
        compiler_params=params(),
        name="pack",
    )(start_state, final_cotangent, diffusivity, donor_map, donor_weight)


def iota(shape, axis):
    return lax.broadcasted_iota(jnp.int32, shape, axis)


def left(x, by=1):
    return pltpu.roll(x, x.shape[-1] - by, x.ndim - 1)


def right(x, by=1):
    return pltpu.roll(x, by, x.ndim - 1)


def stencil(x):
    inn = jnp.where(iota(x.shape, 0) == 0, 0.0, pltpu.roll(x, 1, 0))
    return left(x) + right(x) + pltpu.roll(x, SUB - 1, 0) + inn - 4.0 * x


def strip_forward(u, t, kappa, c):
    new = []
    for v in range(NV):
        reaction = sum(c[v, w] * t[w] for w in range(NV))
        new.append(u[v] + kappa * stencil(u[v]) - reaction)
    return new


def strip_backward(lam, t, kappa, c):
    new = []
    for v in range(NV):
        pulled = sum(c[w, v] * lam[w] for w in range(NV))
        new.append(lam[v] + stencil(kappa * lam[v]) - (1.0 - t[v] * t[v]) * pulled)
    return new


def wall_kernel(own, before, after, c, proj, area, ids, dist, out, sides, *, devices):
    rows, nodes = own.shape[1], area.shape[1]
    for i, ref in enumerate((before, after)):
        for j in range(-(-WALL // WALL_ROWS)):
            a, b = j * WALL_ROWS, min((j + 1) * WALL_ROWS, WALL)
            sides[i, a:b, :] = ref[EDGE_W : EDGE_W + b - a, j * LANES : (j + 1) * LANES]

    def first(start, cols):
        start = start - ROW_K
        piece = jnp.concatenate(
            [ref[start : start + cols, :] for ref in (sides.at[0], own, sides.at[1])], axis=1
        )
        pad = jnp.zeros((SUB - cols, piece.shape[1]), jnp.float32)
        return jnp.concatenate([piece, pad], axis=0)

    kappa = first(ROW_K, UCOLS)
    u = [first(ROW_U + v * UCOLS, UCOLS) for v in range(NV)]
    lam = [first(ROW_L + v * LCOLS, LCOLS) for v in range(NV)]
    history = []
    for n in range(STEPS):
        t = [jnp.tanh(x) for x in u]
        history.append((u, t))
        if n < STEPS - 1:
            u = strip_forward(u, t, kappa, c)
    h = [0.0] * NV
    for n in reversed(range(STEPS)):
        u, t = history[n]
        h = [h[v] + (lam[v] * u[v])[0:1, rows : 2 * rows] for v in range(NV)]
        if n > 0:
            lam = strip_backward(lam, t, kappa, c)
    per_row = nodes // rows
    groups = CP_DEV // LANES
    s_rows = [sum(proj[i // groups, v] * h[v] for v in range(NV)) for i in range(3 * groups)]
    s_rows += [jnp.zeros((SUB - 3 * groups, rows), jnp.float32)]
    spread = (iota((rows, nodes), 1) // per_row == iota((rows, nodes), 0)).astype(jnp.float32)
    s = jnp.dot(
        jnp.concatenate(s_rows, axis=0), spread,
        precision=lax.Precision.HIGHEST, preferred_element_type=jnp.float32,
    )
    s = s * area[...]
    d = dist[0]
    q = 1.0 - d
    q = q * q
    phi = q * q * (4.0 * d + 1.0)
    key = ids[0]
    major, minor = key // LANES, key % LANES
    shape = (devices, SUB, nodes)
    target = iota(shape, 0) * groups + iota(shape, 1) % groups
    total = jnp.zeros((devices * SUB, LANES), jnp.float32)
    bf = jnp.bfloat16
    for k in range(d.shape[0]):
        lo = (iota((LANES, nodes), 0) == minor[k : k + 1]).astype(bf)
        hit = target == major[k : k + 1][None]
        w = s * phi[k : k + 1]
        for piece in range(3):
            part = w.astype(bf).astype(jnp.float32)
            w = w - part
            a = jnp.where(hit, part[None], 0.0).reshape(devices * SUB, nodes).astype(bf)
            total += lax.dot_general(
                a, lo, (((1,), (1,)), ((), ())), preferred_element_type=jnp.float32
            )
    out[...] = total.reshape(devices, SUB, LANES)


def wall_gradient(own, before, after, coupling, proj, area, ids, dist, devices):
    vm = pl.BlockSpec(memory_space=pltpu.VMEM)
    sm = pl.BlockSpec(memory_space=pltpu.SMEM)
    return pl.pallas_call(
        functools.partial(wall_kernel, devices=devices),
        in_specs=[vm, vm, vm, sm, sm, vm, vm, vm],
        out_specs=vm,
        out_shape=jax.ShapeDtypeStruct((devices, SUB, LANES), jnp.float32),
        scratch_shapes=[pltpu.VMEM((2, WALL, own.shape[1]), jnp.float32)],
        compiler_params=params(),
        name="wall_gradient",
    )(own, before, after, coupling, proj, area, ids, dist)


def sum_kernel(parts, out):
    total = parts[...].sum(axis=0)
    groups = CP_DEV // LANES
    for i in range(3 * groups):
        c, g = i // groups, i % groups
        out[c : c + 1, g * LANES : (g + 1) * LANES] = total[i : i + 1]


def sum_points(parts):
    vm = pl.BlockSpec(memory_space=pltpu.VMEM)
    return pl.pallas_call(
        sum_kernel,
        in_specs=[vm],
        out_specs=vm,
        out_shape=jax.ShapeDtypeStruct((3, CP_DEV), jnp.float32),
        compiler_params=params(),
        name="sum_points",
    )(parts)


def face_kernel(same, other, c, out, buf, turned, flip, *, rows):
    block = lax.axis_index("block")
    blocks = same.shape[0] // 2 * 2
    shape = (blocks, LANES)
    for m in range(blocks // 2):
        at = block ^ (2 * m)
        for q in range(2):
            start = q * STRIP * blocks
            buf[pl.ds(start + at, STRIP, stride=blocks), :] = same[2 * m + q]
            buf[pl.ds(start + (at ^ 1), STRIP, stride=blocks), :] = other[2 * m + q]

    def load(q, row):
        return buf[pl.ds((q * STRIP + row) * blocks, blocks), :]

    lane = iota(shape, 1)
    place = (iota(shape, 0) * LANES + lane).astype(jnp.float32)
    size = float(blocks * rows)

    def later(x, by=1):
        y = jnp.where(lane >= by, x, pltpu.roll(x, blocks - 1, 0))
        return pltpu.roll(y, LANES - by, 1)

    def earlier(x, by=1):
        y = jnp.where(lane < LANES - by, x, pltpu.roll(x, 1, 0))
        return pltpu.roll(y, by, 1)

    def later_far(x, whole, rest):
        near = pltpu.roll(x, (blocks - whole) % blocks, 0)
        y = jnp.where(lane >= rest, near, pltpu.roll(near, blocks - 1, 0))
        return pltpu.roll(y, (LANES - rest) % LANES, 1)

    def earlier_far(x, whole, rest):
        near = pltpu.roll(x, whole, 0)
        y = jnp.where(lane < LANES - rest, near, pltpu.roll(near, 1, 0))
        return pltpu.roll(y, rest, 1)

    far, taps = {}, {}
    for q in range(2):
        for n in range(STEPS):
            delta = load(q, n) - place
            delta = jnp.where(delta < 0.0, delta + size, delta)
            start = delta[0:1, 0:1]
            rel = delta - start + float(STEPS)
            rel = jnp.where(rel < 0.0, rel + size, rel)
            rel = jnp.where(rel >= size, rel - size, rel)
            least = jnp.min(jnp.min(rel, axis=0, keepdims=True), axis=1, keepdims=True)
            e = rel - least
            t = start - float(STEPS) + least
            t = jnp.where(t < 0.0, t + size, t)
            t = jnp.where(t >= size, t - size, t).astype(jnp.int32)[0, 0]
            far[q, n] = (t // LANES, t % LANES)
            share = load(q, STEPS + n)
            taps[q, n] = [
                jnp.where(e == float(i), share, 0.0)
                + jnp.where(e == float(i - 1), 1.0 - share, 0.0)
                for i in range(TAPS)
            ]

    def ghost(q, n, faces):
        result = []
        for f in faces:
            f = later_far(f, *far[q, n])
            after = pltpu.roll(f, blocks - 1, 0)
            acc = taps[q, n][0] * f
            for i in range(1, TAPS):
                y = pltpu.roll(jnp.where(lane >= i, f, after), LANES - i, 1)
                acc = acc + taps[q, n][i] * y
            result.append(acc)
        return result

    def back(q, n, faces):
        result = []
        for f in faces:
            here = taps[q, n][0] * f
            carried = jnp.zeros_like(here)
            for i in range(1, TAPS):
                y = pltpu.roll(taps[q, n][i] * f, i, 1)
                here = here + jnp.where(lane >= i, y, 0.0)
                carried = carried + jnp.where(lane < i, y, 0.0)
            result.append(earlier_far(here + pltpu.roll(carried, 1, 0), *far[q, n]))
        return result

    def emit(index, g):
        for v in range(NV):
            turned[pl.ds((index * SUB + v) * blocks, blocks), :] = g[v]

    last = UCOLS - 1
    kappa = [[load(q, ROW_K + k) for k in range(UCOLS)] for q in range(2)]
    u = [
        [{k: load(q, ROW_U + v * UCOLS + k) for k in range(UCOLS)} for v in range(NV)]
        for q in range(2)
    ]
    gap = UCOLS - LCOLS
    lam = [
        [{k: load(q, ROW_L + v * LCOLS + k - gap) for k in range(gap, UCOLS)} for v in range(NV)]
        for q in range(2)
    ]
    history = {}
    for n in range(STEPS):
        first = n + 1 if n < STEPS - 1 else STEPS - 1
        for q in range(2):
            history[n, q] = [
                {k: jnp.tanh(u[q][v][k]) for k in range(first, UCOLS)} for v in range(NV)
            ]
        if n == STEPS - 1:
            break
        g = [ghost(q, n, [u[1 - q][v][last] for v in range(NV)]) for q in range(2)]
        emit(n, g[0])
        new = []
        for q in range(2):
            side = []
            for v in range(NV):
                cols = {}
                for k in range(n + 1, UCOLS):
                    x = u[q][v][k]
                    outer = u[q][v][k + 1] if k < last else g[q][v]
                    lap = later(x) + earlier(x) + u[q][v][k - 1] + outer - 4.0 * x
                    reaction = sum(c[v, w] * history[n, q][w][k] for w in range(NV))
                    cols[k] = x + kappa[q][k] * lap - reaction
                side.append(cols)
            new.append(side)
        u = new
    for n in reversed(range(STEPS)):
        s = [
            [{k: kappa[q][k] * x for k, x in lam[q][v].items()} for v in range(NV)]
            for q in range(2)
        ]
        sides = (0, 1) if n > 1 else (1,) if n == 1 else ()
        g = {
            q: back(1 - q, n, [s[1 - q][v][last] for v in range(NV)]) for q in {0, *sides}
        }
        emit(STEPS - 1 + n, g[0])
        new = [None, None]
        for q in sides:
            side = []
            for v in range(NV):
                cols = {}
                for k in range(UCOLS - n, UCOLS):
                    x = lam[q][v][k]
                    y = s[q][v][k]
                    outer = s[q][v][k + 1] if k < last else g[q][v]
                    lap = later(y) + earlier(y) + s[q][v][k - 1] + outer - 4.0 * y
                    pulled = sum(c[w, v] * lam[q][w][k] for w in range(NV))
                    t = history[n, q][v][k]
                    cols[k] = x + lap - (1.0 - t * t) * pulled
                side.append(cols)
            new[q] = side
        if n == 1:
            new[0] = [{last: jnp.zeros(shape, jnp.float32)} for v in range(NV)]
        lam = new

    count = (2 * STEPS - 1) * SUB
    flip[...] = jnp.zeros_like(flip)
    around = [
        turned[pl.ds(lax.rem(block + shift + blocks, blocks), count, stride=blocks), :]
        for shift in (-1, 0, 1)
    ]
    wide = jnp.concatenate(around, axis=1)
    wide = pltpu.roll(wide, wide.shape[1] - (LANES - HALO), 1)
    flip[0:count, :] = wide[:, : 2 * LANES]
    for j in range(2):
        out[j * LANES : (j + 1) * LANES, :] = flip[:, j * LANES : (j + 1) * LANES].T


def face_terms(same, other, coupling, rows):
    vm = pl.BlockSpec(memory_space=pltpu.VMEM)
    sm = pl.BlockSpec(memory_space=pltpu.SMEM)
    blocks = same.shape[0]
    f32 = jnp.float32
    return pl.pallas_call(
        functools.partial(face_kernel, rows=rows),
        in_specs=[vm, vm, sm],
        out_specs=vm,
        out_shape=jax.ShapeDtypeStruct((2 * LANES, LANES), f32),
        scratch_shapes=[
            pltpu.VMEM((2 * STRIP * blocks, LANES), f32),
            pltpu.VMEM(((2 * STEPS - 1) * SUB * blocks, LANES), f32),
            pltpu.VMEM((LANES, 2 * LANES), f32),
        ],
        compiler_params=params(),
        name="face_terms",
    )(same, other, coupling)


def field_kernel(
    u_hbm, l_hbm, k_hbm, before, after, terms, c, out,
    ext_u, ext_l, ext_k, kap, states, tanhs, lam, scaled, sems,
):
    rows, radial = u_hbm.shape[2], u_hbm.shape[3]
    chunks = kap.shape[0]
    tiles = radial // LANES
    own = pl.ds(HALO, rows)

    def cut(j):
        return slice(j * LANES, (j + 1) * LANES)

    copies = []
    for j in range(tiles):
        lanes = pl.ds(j * LANES, LANES)
        copies += [
            pltpu.make_async_copy(u_hbm.at[:, 0, :, lanes], ext_u.at[:, j, own], sems.at[0, j]),
            pltpu.make_async_copy(l_hbm.at[:, 0, :, lanes], ext_l.at[:, j, own], sems.at[1, j]),
            pltpu.make_async_copy(k_hbm.at[0, :, lanes], ext_k.at[j, own], sems.at[2, j]),
        ]
    for copy in copies:
        copy.start()
    for ref, lower in ((before, True), (after, False)):
        start = 0 if lower else HALO + rows
        at = start + HALO - UCOLS if lower else start
        below = start + HALO - LCOLS if lower else start
        for j in range(tiles):
            for v in range(NV):
                ext_u[v, j, start : start + HALO] = jnp.zeros((HALO, LANES), jnp.float32)
                ext_l[v, j, start : start + HALO] = jnp.zeros((HALO, LANES), jnp.float32)
                ext_u[v, j, at : at + UCOLS] = ref[v * UCOLS : (v + 1) * UCOLS, cut(j)]
                ext_l[v, j, below : below + LCOLS] = ref[
                    EDGE_L + v * LCOLS : EDGE_L + (v + 1) * LCOLS, cut(j)
                ]
            ext_k[j, start : start + HALO] = jnp.zeros((HALO, LANES), jnp.float32)
            ext_k[j, at : at + UCOLS] = ref[EDGE_K:EDGE_W, cut(j)]
    for copy in copies:
        copy.wait()

    def load(i, carry):
        at = pl.ds(i, SUB, stride=chunks)
        for j in range(tiles):
            kappa = ext_k[j, at, :]
            kap[i, :, cut(j)] = kappa
            for v in range(NV):
                states[0, v, i + 1, :, cut(j)] = ext_u[v, j, at, :]
                x = ext_l[v, j, at, :]
                lam[v, i, :, cut(j)] = x
                scaled[0, v, i + 1, :, cut(j)] = kappa * x
        return carry

    lax.fori_loop(0, chunks, load, 0, unroll=2)

    def wrap(ref):
        for v in range(NV):
            ref[v, 0] = pltpu.roll(ref[v, chunks], 1, 0)
            ref[v, chunks + 1] = pltpu.roll(ref[v, 1], SUB - 1, 0)

    wrap(states.at[0])
    wrap(scaled.at[0])
    lane = iota((SUB, LANES), 1)
    is_first, is_last = lane == 0, lane == LANES - 1

    def neighbours(ref, v, i, j, edge, cache):
        def tile(b):
            if (v, b) not in cache:
                x = ref[v, i + 1, :, cut(b)]
                cache[v, b] = (x, pltpu.roll(x, 1, 1), pltpu.roll(x, LANES - 1, 1))
            return cache[v, b]

        x, r, l = tile(j)
        inn = jnp.where(is_first, tile(j - 1)[1] if j > 0 else 0.0, r)
        outv = jnp.where(is_last, tile(j + 1)[2] if j < tiles - 1 else edge, l)
        return ref[v, i, :, cut(j)] + ref[v, i + 2, :, cut(j)] + inn + outv, x

    def edges(i, n):
        e = terms[pl.ds(i, SUB, stride=chunks), :]
        return [pltpu.roll(e, (2 * LANES - 1 - (n * SUB + v)) % LANES, 1) for v in range(NV)]

    def forward(n):
        def body(i, carry):
            edge = edges(i, n)
            cache = {}
            for j in range(tiles):
                kappa = kap[i, :, cut(j)]
                pairs = [neighbours(states.at[n], v, i, j, edge[v], cache) for v in range(NV)]
                t = [jnp.tanh(x) for _, x in pairs]
                for v in range(NV):
                    around, x = pairs[v]
                    tanhs[n, v, i, :, cut(j)] = t[v]
                    reaction = sum(c[v, w] * t[w] for w in range(NV))
                    states[n + 1, v, i + 1, :, cut(j)] = (
                        x + kappa * (around - 4.0 * x) - reaction
                    )
            return carry

        lax.fori_loop(0, chunks, body, 0, unroll=6)
        if n + 1 < STEPS - 1:
            wrap(states.at[n + 1])

    def backward(n, source, target):
        def body(i, carry):
            edge = edges(i, STEPS - 1 + n)
            cache = {}
            for j in range(tiles):
                kappa = kap[i, :, cut(j)]
                pairs = [neighbours(scaled.at[source], v, i, j, edge[v], cache) for v in range(NV)]
                x = [lam[v, i, :, cut(j)] for v in range(NV)]
                for v in range(NV):
                    if n < STEPS - 1:
                        t = tanhs[n, v, i, :, cut(j)]
                    else:
                        t = jnp.tanh(states[n, v, i + 1, :, cut(j)])
                    around, s = pairs[v]
                    pulled = sum(c[w, v] * x[w] for w in range(NV))
                    new = x[v] + (around - 4.0 * s) - (1.0 - t * t) * pulled
                    if n > 0:
                        lam[v, i, :, cut(j)] = new
                        scaled[target, v, i + 1, :, cut(j)] = kappa * new
                    else:
                        ext_l[v, j, pl.ds(i, SUB, stride=chunks), :] = new
            return carry

        lax.fori_loop(0, chunks, body, 0, unroll=6)
        if n > 0:
            wrap(scaled.at[target])

    for n in range(STEPS - 1):
        forward(n)
    source = 0
    for n in reversed(range(STEPS)):
        backward(n, source, 1 - source)
        source = 1 - source
    copies = [
        pltpu.make_async_copy(
            ext_l.at[:, j, own], out.at[:, 0, :, pl.ds(j * LANES, LANES)], sems.at[3, j]
        )
        for j in range(tiles)
    ]
    for copy in copies:
        copy.start()
    for copy in copies:
        copy.wait()


def field(start_state, final_cotangent, diffusivity, before, after, terms, coupling):
    _, _, rows, radial = start_state.shape
    ext = rows + 2 * HALO
    chunks, tiles = ext // SUB, radial // LANES
    vm = pl.BlockSpec(memory_space=pltpu.VMEM)
    hbm = pl.BlockSpec(memory_space=pl.ANY)
    f32 = jnp.float32
    return pl.pallas_call(
        field_kernel,
        in_specs=[hbm, hbm, hbm, vm, vm, vm, pl.BlockSpec(memory_space=pltpu.SMEM)],
        out_specs=hbm,
        out_shape=jax.ShapeDtypeStruct(start_state.shape, f32),
        scratch_shapes=[
            pltpu.VMEM((NV, tiles, ext, LANES), f32),
            pltpu.VMEM((NV, tiles, ext, LANES), f32),
            pltpu.VMEM((tiles, ext, LANES), f32),
            pltpu.VMEM((chunks, SUB, radial), f32),
            pltpu.VMEM((STEPS, NV, chunks + 2, SUB, radial), f32),
            pltpu.VMEM((STEPS - 1, NV, chunks, SUB, radial), f32),
            pltpu.VMEM((NV, chunks, SUB, radial), f32),
            pltpu.VMEM((2, NV, chunks + 2, SUB, radial), f32),
            pltpu.SemaphoreType.DMA((4, tiles)),
        ],
        compiler_params=params(),
        name="field",
    )(start_state, final_cotangent, diffusivity, before, after, terms, coupling)


def ring(x, step):
    size = lax.axis_size("block")
    return lax.ppermute(x, "block", [(i, (i + step) % size) for i in range(size)])


def crossed(x, mask):
    return lax.ppermute(x, "block", [(i, i ^ mask) for i in range(lax.axis_size("block"))])


def swapped(x):
    return lax.ppermute(x, "zone", [(i, i ^ 1) for i in range(lax.axis_size("zone"))])


def gather_pair(strip):
    x = jnp.stack([strip, swapped(strip)])
    bit, size = 1, lax.axis_size("block")
    while 2**bit < size:
        wide = 4 if 2 ** (bit + 1) < size else 2
        x = jnp.concatenate([x] + [crossed(x, k << bit) for k in range(1, wide)], axis=0)
        bit += 2 if wide == 4 else 1
    return x, crossed(x, 1)


def local(
    start_state,
    diffusivity,
    donor_map,
    donor_weight,
    coupling,
    final_cotangent,
    wall_area,
    wall_projection,
    center_ids,
    center_dist,
):
    rows = start_state.shape[2]
    devices = lax.axis_size("zone") * lax.axis_size("block")
    strip, wall, low, high = pack(
        start_state, final_cotangent, diffusivity, donor_map, donor_weight
    )
    before, after = ring(high, 1), ring(low, -1)
    same, other = gather_pair(strip)
    points = wall_gradient(
        wall, before, after, coupling, wall_projection, wall_area, center_ids, center_dist, devices
    )
    points = lax.all_to_all(points, ("zone", "block"), 0, 0, tiled=True)
    gradient = sum_points(points)
    terms = face_terms(same, other, coupling, rows)
    adjoint = field(start_state, final_cotangent, diffusivity, before, after, terms, coupling)
    return adjoint, gradient


def solution(mesh):
    return jax.shard_map(
        local,
        mesh=mesh,
        in_specs=(
            P(None, "zone", "block", None),
            P("zone", "block", None),
            P(None, "zone", None),
            P(None, "zone", None),
            P(),
            P(None, "zone", "block", None),
            P("zone", "block"),
            P(),
            P("zone", None, "block"),
            P("zone", None, "block"),
        ),
        out_specs=(P(None, "zone", "block", None), P(None, ("zone", "block"))),
        check_vma=False,
    )
```

```python
import functools

import jax
import jax.numpy as jnp
from jax import lax
from jax.experimental import pallas as pl
from jax.experimental.pallas import tpu as pltpu
from jax.sharding import PartitionSpec as P

CP_DEV = 256
LANES = 128
SUB = 8
STEPS = 4
NV = 5
UCOLS = STEPS + 2
LCOLS = STEPS
HALO = SUB
ROW_K = 2 * STEPS
ROW_U = ROW_K + UCOLS
ROW_L = ROW_U + NV * UCOLS
STRIP = ROW_L + NV * LCOLS
EDGE_L = NV * UCOLS
EDGE_K = EDGE_L + NV * LCOLS
EDGE = EDGE_K + UCOLS
TAPS = 6
UNROLL = 18
VMEM_LIMIT = 48 * 1024 * 1024


def params(limit=VMEM_LIMIT):
    return pltpu.CompilerParams(vmem_limit_bytes=limit)


def pack_kernel(
    u_hbm, l_hbm, k_hbm, map_hbm, weight_hbm, strip, near, far,
    u_side, l_side, k_side, u_edge, l_edge, k_edge, dmap, dweight, sems,
):
    rows, radial = u_hbm.shape[2], u_hbm.shape[3]
    block = lax.axis_index("block")
    own = pl.ds(pl.multiple_of(block * rows, LANES), rows)
    copies = [
        pltpu.make_async_copy(map_hbm.at[:, 0, own], dmap, sems.at[0, 0]),
        pltpu.make_async_copy(weight_hbm.at[:, 0, own], dweight, sems.at[0, 1]),
    ]
    lanes = pl.ds(radial - LANES, LANES)
    copies += [
        pltpu.make_async_copy(u_hbm.at[:, 0, :, lanes], u_side, sems.at[1, 0]),
        pltpu.make_async_copy(l_hbm.at[:, 0, :, lanes], l_side, sems.at[2, 0]),
        pltpu.make_async_copy(k_hbm.at[0, :, lanes], k_side, sems.at[3, 0]),
    ]
    lower = block % 2 == 0
    top = jnp.where(lower, rows - SUB, 0)
    for i, start in enumerate((top, rows - SUB - top)):
        some = pl.ds(pl.multiple_of(start, SUB), SUB)
        copies += [
            pltpu.make_async_copy(u_hbm.at[:, 0, some], u_edge.at[i], sems.at[4, i]),
            pltpu.make_async_copy(l_hbm.at[:, 0, some], l_edge.at[i], sems.at[5, i]),
            pltpu.make_async_copy(k_hbm.at[0, some], k_edge.at[i], sems.at[6, i]),
        ]
    for copy in copies:
        copy.start()
    for copy in copies:
        copy.wait()
    strip[0:STEPS, :] = dmap[...].astype(jnp.float32)
    strip[STEPS : 2 * STEPS, :] = dweight[...]
    strip[ROW_K : ROW_K + UCOLS, :] = k_side[...].T[LANES - UCOLS :]
    for v in range(NV):
        a, b = ROW_U + v * UCOLS, ROW_L + v * LCOLS
        strip[a : a + UCOLS, :] = u_side[v].T[LANES - UCOLS :]
        strip[b : b + LCOLS, :] = l_side[v].T[LANES - LCOLS :]
    for i, ref in enumerate((near, far)):
        last = lower if i == 0 else jnp.logical_not(lower)

        def ends(x, count):
            return jnp.where(last, x[SUB - count :], x[:count])

        for v in range(NV):
            ref[v * UCOLS : (v + 1) * UCOLS, :] = ends(u_edge[i, v], UCOLS)
            ref[EDGE_L + v * LCOLS : EDGE_L + (v + 1) * LCOLS, :] = ends(l_edge[i, v], LCOLS)
        ref[EDGE_K:EDGE, :] = ends(k_edge[i], UCOLS)


def pack(start_state, final_cotangent, diffusivity, donor_map, donor_weight):
    _, _, rows, radial = start_state.shape
    f32 = jnp.float32
    outs = ((STRIP, rows), (EDGE, radial), (EDGE, radial))
    return pl.pallas_call(
        pack_kernel,
        in_specs=[pl.BlockSpec(memory_space=pltpu.HBM)] * 5,
        out_specs=[pl.BlockSpec(memory_space=pltpu.VMEM)] * 3,
        out_shape=[jax.ShapeDtypeStruct(s, f32) for s in outs],
        scratch_shapes=[
            pltpu.VMEM((NV, rows, LANES), f32),
            pltpu.VMEM((NV, rows, LANES), f32),
            pltpu.VMEM((rows, LANES), f32),
            pltpu.VMEM((2, NV, SUB, radial), f32),
            pltpu.VMEM((2, NV, SUB, radial), f32),
            pltpu.VMEM((2, SUB, radial), f32),
            pltpu.VMEM((STEPS, rows), jnp.int32),
            pltpu.VMEM((STEPS, rows), f32),
            pltpu.SemaphoreType.DMA((7, 2)),
        ],
        compiler_params=params(),
        name="pack",
    )(
        *(
            pltpu.with_memory_space_constraint(x, pltpu.HBM)
            for x in (start_state, final_cotangent, diffusivity, donor_map, donor_weight)
        )
    )


def iota(shape, axis):
    return lax.broadcasted_iota(jnp.int32, shape, axis)


def left(x, by=1):
    return pltpu.roll(x, x.shape[-1] - by, x.ndim - 1)


def right(x, by=1):
    return pltpu.roll(x, by, x.ndim - 1)


def stencil(x):
    inn = jnp.where(iota(x.shape, 0) == 0, 0.0, pltpu.roll(x, 1, 0))
    return left(x) + right(x) + pltpu.roll(x, SUB - 1, 0) + inn - 4.0 * x


def strip_forward(u, t, kappa, c):
    new = []
    for v in range(NV):
        reaction = sum(c[v, w] * t[w] for w in range(NV))
        new.append(u[v] + kappa * stencil(u[v]) - reaction)
    return new


def strip_backward(lam, t, kappa, c):
    new = []
    for v in range(NV):
        pulled = sum(c[w, v] * lam[w] for w in range(NV))
        new.append(lam[v] + stencil(kappa * lam[v]) - (1.0 - t[v] * t[v]) * pulled)
    return new


def wall_kernel(
    u_own, l_own, k_own, near, far, c_hbm, proj, area, ids, dist, out, c, sem, *, devices
):
    rows, nodes = u_own.shape[2], area.shape[1]
    copy = pltpu.make_async_copy(c_hbm, c, sem)
    copy.start()
    lower = lax.axis_index("block") % 2 == 0
    x, y = near[:, 0:LANES], far[:, 0:LANES]
    gap = jnp.zeros((LANES - 2 * EDGE, LANES), jnp.float32)
    halos = jnp.concatenate([jnp.where(lower, y, x), jnp.where(lower, x, y), gap], axis=0).T[:SUB]
    lane = iota((SUB, LANES), 1)

    def first(own, edge, cols):
        after = pltpu.roll(halos, (LANES - EDGE - edge) % LANES, 1)
        before = pltpu.roll(halos, (LANES - cols - edge) % LANES, 1)
        beside = jnp.where(lane < cols, after, jnp.where(lane >= LANES - cols, before, 0.0))
        return jnp.concatenate([own[:, :LANES].T[:SUB], beside], axis=1)

    kappa = first(k_own.at[0], EDGE_K, UCOLS)
    u = [first(u_own.at[v, 0], v * UCOLS, UCOLS) for v in range(NV)]
    lam = [first(l_own.at[v, 0], EDGE_L + v * LCOLS, LCOLS) for v in range(NV)]
    copy.wait()
    history = []
    for n in range(STEPS):
        t = [jnp.tanh(x) for x in u]
        history.append((u, t))
        if n < STEPS - 1:
            u = strip_forward(u, t, kappa, c)
    h = [0.0] * NV
    for n in reversed(range(STEPS)):
        u, t = history[n]
        h = [h[v] + (lam[v] * u[v])[0:1, :rows] for v in range(NV)]
        if n > 0:
            lam = strip_backward(lam, t, kappa, c)
    per_row = nodes // rows
    groups = CP_DEV // LANES
    s_rows = [sum(proj[i // groups, v] * h[v] for v in range(NV)) for i in range(3 * groups)]
    s_rows += [jnp.zeros((SUB - 3 * groups, rows), jnp.float32)]
    spread = (iota((rows, nodes), 1) // per_row == iota((rows, nodes), 0)).astype(jnp.float32)
    s = jnp.dot(
        jnp.concatenate(s_rows, axis=0), spread,
        precision=lax.Precision.HIGHEST, preferred_element_type=jnp.float32,
    )
    s = s * area[...]
    d = dist[0]
    q = 1.0 - d
    q = q * q
    phi = q * q * (4.0 * d + 1.0)
    key = ids[0]
    major, minor = key // LANES, key % LANES
    shape = (devices, SUB, nodes)
    target = iota(shape, 0) * groups + iota(shape, 1) % groups
    total = jnp.zeros((devices * SUB, LANES), jnp.float32)
    bf = jnp.bfloat16
    for k in range(d.shape[0]):
        lo = (iota((LANES, nodes), 0) == minor[k : k + 1]).astype(bf)
        hit = target == major[k : k + 1][None]
        w = s * phi[k : k + 1]
        for piece in range(2):
            part = w.astype(bf).astype(jnp.float32)
            w = w - part
            a = jnp.where(hit, part[None], 0.0).reshape(devices * SUB, nodes).astype(bf)
            total += lax.dot_general(
                a, lo, (((1,), (1,)), ((), ())), preferred_element_type=jnp.float32
            )
    out[...] = total.reshape(devices, SUB, LANES)


def wall_gradient(u, lam, kappa, near, far, coupling, proj, area, ids, dist, devices):
    vm = pl.BlockSpec(memory_space=pltpu.VMEM)
    sm = pl.BlockSpec(memory_space=pltpu.SMEM)
    return pl.pallas_call(
        functools.partial(wall_kernel, devices=devices),
        in_specs=[vm] * 5 + [pl.BlockSpec(memory_space=pltpu.HBM), sm, vm, vm, vm],
        out_specs=vm,
        out_shape=jax.ShapeDtypeStruct((devices, SUB, LANES), jnp.float32),
        scratch_shapes=[pltpu.SMEM(coupling.shape, jnp.float32), pltpu.SemaphoreType.DMA],
        compiler_params=params(),
        name="wall_gradient",
    )(u, lam, kappa, near, far, coupling, proj, area, ids, dist)


def sum_kernel(parts, out):
    total = parts[...].sum(axis=0)
    groups = CP_DEV // LANES
    for i in range(3 * groups):
        c, g = i // groups, i % groups
        out[c : c + 1, g * LANES : (g + 1) * LANES] = total[i : i + 1]


def sum_points(parts):
    vm = pl.BlockSpec(memory_space=pltpu.VMEM)
    return pl.pallas_call(
        sum_kernel,
        in_specs=[vm],
        out_specs=vm,
        out_shape=jax.ShapeDtypeStruct((3, CP_DEV), jnp.float32),
        compiler_params=params(),
        name="sum_points",
    )(parts)


def face_terms(same, other, c, out, buf, turned, flip, rows, ready):
    block = lax.axis_index("block")
    blocks = 2 * same[0].shape[0]
    shape = (blocks, LANES)
    for m in range(blocks // 2):
        at = block ^ (2 * m)
        for q in range(2):
            start = q * STRIP * blocks
            buf[pl.ds(start + at, STRIP, stride=blocks), :] = same[q][m]
            buf[pl.ds(start + (at ^ 1), STRIP, stride=blocks), :] = other[q][m]

    def load(q, row):
        return buf[pl.ds((q * STRIP + row) * blocks, blocks), :]

    lane = iota(shape, 1)
    place = (iota(shape, 0) * LANES + lane).astype(jnp.float32)
    size = float(blocks * rows)

    def later(x, by=1):
        y = jnp.where(lane >= by, x, pltpu.roll(x, blocks - 1, 0))
        return pltpu.roll(y, LANES - by, 1)

    def earlier(x, by=1):
        y = jnp.where(lane < LANES - by, x, pltpu.roll(x, 1, 0))
        return pltpu.roll(y, by, 1)

    far, taps = {}, {}
    for q in range(2):
        for n in range(STEPS):
            delta = load(q, n) - place
            delta = jnp.where(delta < 0.0, delta + size, delta)
            start = delta[0:1, 0:1]
            rel = delta - start + float(STEPS)
            rel = jnp.where(rel < 0.0, rel + size, rel)
            rel = jnp.where(rel >= size, rel - size, rel)
            least = jnp.min(jnp.min(rel, axis=0, keepdims=True), axis=1, keepdims=True)
            e = rel - least
            t = start - float(STEPS) + least
            t = jnp.where(t < 0.0, t + size, t)
            t = jnp.where(t >= size, t - size, t).astype(jnp.int32)[0, 0]
            far[q, n] = (t // LANES, t % LANES)
            share = load(q, STEPS + n)
            taps[q, n] = [
                jnp.where(e == float(i), share, 0.0)
                + jnp.where(e == float(i - 1), 1.0 - share, 0.0)
                for i in range(TAPS)
            ]

    def shifts(q, n):
        whole, rest = far[q, n]
        return whole, [
            (jnp.where(rest + i < LANES, rest + i, rest + i - LANES), lane >= rest + i,
             lane >= rest + i - LANES)
            for i in range(TAPS)
        ]

    def ghost(q, n, faces):
        whole, moves = shifts(q, n)
        result = []
        for f in faces:
            near = [pltpu.roll(f, (2 * blocks - whole - k) % blocks, 0) for k in range(3)]
            acc = 0.0
            for i, (by, here, next_one) in enumerate(moves):
                y = jnp.where(here, near[0], jnp.where(next_one, near[1], near[2]))
                acc = acc + taps[q, n][i] * pltpu.roll(y, (LANES - by) % LANES, 1)
            result.append(acc)
        return result

    def back(q, n, faces):
        whole, moves = shifts(q, n)
        result = []
        for f in faces:
            parts = [0.0, 0.0, 0.0]
            for i, (by, here, next_one) in enumerate(moves):
                y = pltpu.roll(taps[q, n][i] * f, by, 1)
                parts[0] = parts[0] + jnp.where(here, y, 0.0)
                parts[1] = parts[1] + jnp.where(here, 0.0, jnp.where(next_one, y, 0.0))
                parts[2] = parts[2] + jnp.where(next_one, 0.0, y)
            result.append(
                sum(pltpu.roll(parts[k], (whole + k) % blocks, 0) for k in range(3))
            )
        return result

    def emit(index, g):
        for v in range(NV):
            turned[pl.ds((index * SUB + v) * blocks, blocks), :] = g[v]

    last = UCOLS - 1
    kappa = [[load(q, ROW_K + k) for k in range(UCOLS)] for q in range(2)]
    u = [
        [{k: load(q, ROW_U + v * UCOLS + k) for k in range(UCOLS)} for v in range(NV)]
        for q in range(2)
    ]
    gap = UCOLS - LCOLS
    lam = [
        [{k: load(q, ROW_L + v * LCOLS + k - gap) for k in range(gap, UCOLS)} for v in range(NV)]
        for q in range(2)
    ]
    history = {}
    ready()
    for n in range(STEPS):
        first = n + 1 if n < STEPS - 1 else STEPS - 1
        for q in range(2):
            history[n, q] = [
                {k: jnp.tanh(u[q][v][k]) for k in range(first, UCOLS)} for v in range(NV)
            ]
        if n == STEPS - 1:
            break
        g = [ghost(q, n, [u[1 - q][v][last] for v in range(NV)]) for q in range(2)]
        emit(n, g[0])
        new = []
        for q in range(2):
            side = []
            for v in range(NV):
                cols = {}
                for k in range(n + 1, UCOLS):
                    x = u[q][v][k]
                    outer = u[q][v][k + 1] if k < last else g[q][v]
                    lap = later(x) + earlier(x) + u[q][v][k - 1] + outer - 4.0 * x
                    reaction = sum(c[v, w] * history[n, q][w][k] for w in range(NV))
                    cols[k] = x + kappa[q][k] * lap - reaction
                side.append(cols)
            new.append(side)
        u = new
    for n in reversed(range(STEPS)):
        s = [
            [{k: kappa[q][k] * x for k, x in lam[q][v].items()} for v in range(NV)]
            for q in range(2)
        ]
        sides = (0, 1) if n > 1 else (1,) if n == 1 else ()
        g = {
            q: back(1 - q, n, [s[1 - q][v][last] for v in range(NV)]) for q in {0, *sides}
        }
        emit(STEPS - 1 + n, g[0])
        new = [None, None]
        for q in sides:
            side = []
            for v in range(NV):
                cols = {}
                for k in range(UCOLS - n, UCOLS):
                    x = lam[q][v][k]
                    y = s[q][v][k]
                    outer = s[q][v][k + 1] if k < last else g[q][v]
                    lap = later(y) + earlier(y) + s[q][v][k - 1] + outer - 4.0 * y
                    pulled = sum(c[w, v] * lam[q][w][k] for w in range(NV))
                    t = history[n, q][v][k]
                    cols[k] = x + lap - (1.0 - t * t) * pulled
                side.append(cols)
            new[q] = side
        if n == 1:
            new[0] = [{last: jnp.zeros(shape, jnp.float32)} for v in range(NV)]
        lam = new

    count = (2 * STEPS - 1) * SUB
    flip[...] = jnp.zeros_like(flip)
    around = [
        turned[pl.ds(lax.rem(block + shift + blocks, blocks), count, stride=blocks), :]
        for shift in (-1, 0, 1)
    ]
    wide = jnp.concatenate(around, axis=1)
    wide = pltpu.roll(wide, wide.shape[1] - (LANES - HALO), 1)
    flip[0:count, :] = wide[:, : 2 * LANES]
    for j in range(2):
        out[j * LANES : (j + 1) * LANES, :] = flip[:, j * LANES : (j + 1) * LANES].T


def field_kernel(
    u_hbm, l_hbm, k_hbm, near, far, same_0, same_1, other_0, other_1, c_hbm, out,
    c, ext_u, ext_l, ext_k, kap, rest, states, tanhs, lam, scaled, terms, buf, turned, flip, sems,
):
    rows, radial = u_hbm.shape[2], u_hbm.shape[3]
    chunks = kap.shape[0]
    tiles = radial // LANES
    own = pl.ds(HALO, rows)

    def cut(j):
        return slice(j * LANES, (j + 1) * LANES)

    c_copy = pltpu.make_async_copy(c_hbm, c, sems.at[4, 0])
    c_copy.start()
    copies = []
    for j in range(tiles):
        lanes = pl.ds(j * LANES, LANES)
        copies += [
            pltpu.make_async_copy(u_hbm.at[:, 0, :, lanes], ext_u.at[:, j, own], sems.at[0, j]),
            pltpu.make_async_copy(l_hbm.at[:, 0, :, lanes], ext_l.at[:, j, own], sems.at[1, j]),
            pltpu.make_async_copy(k_hbm.at[0, :, lanes], ext_k.at[j, own], sems.at[2, j]),
        ]
    for copy in copies:
        copy.start()
    face_terms(
        (same_0, same_1), (other_0, other_1), c, terms, buf, turned, flip, rows, c_copy.wait
    )
    lower = lax.axis_index("block") % 2 == 0

    def halo(a, b, cols):
        x, y = near[a:b, cols], far[a:b, cols]
        return jnp.where(lower, y, x), jnp.where(lower, x, y)

    def put(ref, where, pair, count):
        gap = jnp.zeros((HALO - count, LANES), jnp.float32)
        ref[(*where, pl.ds(0, HALO))] = jnp.concatenate([gap, pair[0]], axis=0)
        ref[(*where, pl.ds(HALO + rows, HALO))] = jnp.concatenate([pair[1], gap], axis=0)

    for j in range(tiles):
        put(ext_k, (j,), halo(EDGE_K, EDGE, cut(j)), UCOLS)
        for v in range(NV):
            put(ext_u, (v, j), halo(v * UCOLS, (v + 1) * UCOLS, cut(j)), UCOLS)
            at = EDGE_L + v * LCOLS
            put(ext_l, (v, j), halo(at, at + LCOLS, cut(j)), LCOLS)
    for copy in copies:
        copy.wait()

    def load(i, carry):
        at = pl.ds(i, SUB, stride=chunks)
        for j in range(tiles):
            kappa = ext_k[j, at, :]
            kap[i, :, cut(j)] = kappa
            rest[i, :, cut(j)] = 1.0 - 4.0 * kappa
            for v in range(NV):
                states[0, v, i + 1, :, cut(j)] = ext_u[v, j, at, :]
                x = ext_l[v, j, at, :]
                lam[v, i, :, cut(j)] = x
                scaled[0, v, i + 1, :, cut(j)] = kappa * x
        return carry

    lax.fori_loop(0, chunks, load, 0, unroll=2)

    def wrap(ref):
        for v in range(NV):
            ref[v, 0] = pltpu.roll(ref[v, chunks], 1, 0)
            ref[v, chunks + 1] = pltpu.roll(ref[v, 1], SUB - 1, 0)

    wrap(states.at[0])
    wrap(scaled.at[0])
    lane = iota((SUB, LANES), 1)
    is_first, is_last = lane == 0, lane == LANES - 1

    def neighbours(ref, v, i, j, edge, cache):
        def tile(b):
            if (v, b) not in cache:
                x = ref[v, i + 1, :, cut(b)]
                cache[v, b] = (x, pltpu.roll(x, 1, 1), pltpu.roll(x, LANES - 1, 1))
            return cache[v, b]

        x, r, l = tile(j)
        inn = jnp.where(is_first, tile(j - 1)[1] if j > 0 else 0.0, r)
        outv = jnp.where(is_last, tile(j + 1)[2] if j < tiles - 1 else edge, l)
        return ref[v, i, :, cut(j)] + ref[v, i + 2, :, cut(j)] + inn + outv, x

    def edges(i, n):
        e = terms[pl.ds(i, SUB, stride=chunks), :]
        return [pltpu.roll(e, (2 * LANES - 1 - (n * SUB + v)) % LANES, 1) for v in range(NV)]

    def forward(n):
        def body(i, carry):
            edge = edges(i, n)
            cache = {}
            for j in range(tiles):
                kappa = kap[i, :, cut(j)]
                pairs = [neighbours(states.at[n], v, i, j, edge[v], cache) for v in range(NV)]
                t = [jnp.tanh(x) for _, x in pairs]
                for v in range(NV):
                    around, x = pairs[v]
                    tanhs[n, v, i, :, cut(j)] = t[v]
                    reaction = sum(c[v, w] * t[w] for w in range(NV))
                    states[n + 1, v, i + 1, :, cut(j)] = (
                        rest[i, :, cut(j)] * x + kappa * around - reaction
                    )
            return carry

        lax.fori_loop(0, chunks, body, 0, unroll=UNROLL)
        if n + 1 < STEPS - 1:
            wrap(states.at[n + 1])

    def backward(n, source, target, chosen):
        def body(i, carry):
            edge = edges(i, STEPS - 1 + n)
            cache = {}
            for j in range(tiles):
                kappa = kap[i, :, cut(j)]
                x = [lam[v, i, :, cut(j)] for v in range(NV)]
                for v in chosen:
                    around, _ = neighbours(scaled.at[source], v, i, j, edge[v], cache)
                    if n < STEPS - 1:
                        t = tanhs[n, v, i, :, cut(j)]
                    else:
                        t = jnp.tanh(states[n, v, i + 1, :, cut(j)])
                    pulled = sum(c[w, v] * x[w] for w in range(NV))
                    new = rest[i, :, cut(j)] * x[v] + around - (1.0 - t * t) * pulled
                    if n > 0:
                        lam[v, i, :, cut(j)] = new
                        scaled[target, v, i + 1, :, cut(j)] = kappa * new
                    else:
                        ext_l[v, j, pl.ds(i, SUB, stride=chunks), :] = new
            return carry

        lax.fori_loop(0, chunks, body, 0, unroll=UNROLL)
        if n > 0:
            wrap(scaled.at[target])

    for n in range(STEPS - 1):
        forward(n)
    source = 0
    for n in reversed(range(1, STEPS)):
        backward(n, source, 1 - source, range(NV))
        source = 1 - source
    copies = []
    for v in range(NV):
        backward(0, source, 1 - source, (v,))
        for j in range(tiles):
            lanes = pl.ds(j * LANES, LANES)
            copies.append(
                pltpu.make_async_copy(
                    ext_l.at[v, j, own], out.at[v, 0, :, lanes], sems.at[5 + v, j]
                )
            )
            copies[-1].start()
    for copy in copies:
        copy.wait()


def field(start_state, final_cotangent, diffusivity, near, far, strips, coupling):
    _, _, rows, radial = start_state.shape
    ext = rows + 2 * HALO
    chunks, tiles, blocks = ext // SUB, radial // LANES, 2 * strips[0].shape[0]
    vm = pl.BlockSpec(memory_space=pltpu.VMEM)
    hbm = pl.BlockSpec(memory_space=pltpu.HBM)
    f32 = jnp.float32
    return pl.pallas_call(
        field_kernel,
        in_specs=[vm] * 9 + [hbm],
        out_specs=hbm,
        out_shape=jax.ShapeDtypeStruct(start_state.shape, f32),
        scratch_shapes=[
            pltpu.SMEM(coupling.shape, f32),
            pltpu.VMEM((NV, tiles, ext, LANES), f32),
            pltpu.VMEM((NV, tiles, ext, LANES), f32),
            pltpu.VMEM((tiles, ext, LANES), f32),
            pltpu.VMEM((chunks, SUB, radial), f32),
            pltpu.VMEM((chunks, SUB, radial), f32),
            pltpu.VMEM((STEPS, NV, chunks + 2, SUB, radial), f32),
            pltpu.VMEM((STEPS - 1, NV, chunks, SUB, radial), f32),
            pltpu.VMEM((NV, chunks, SUB, radial), f32),
            pltpu.VMEM((2, NV, chunks + 2, SUB, radial), f32),
            pltpu.VMEM((2 * LANES, LANES), f32),
            pltpu.VMEM((2 * STRIP * blocks, LANES), f32),
            pltpu.VMEM(((2 * STEPS - 1) * SUB * blocks, LANES), f32),
            pltpu.VMEM((LANES, 2 * LANES), f32),
            pltpu.SemaphoreType.DMA((5 + NV, tiles)),
        ],
        compiler_params=params(),
        name="field",
    )(start_state, final_cotangent, diffusivity, near, far, *strips, coupling)


def beyond(x):
    size = lax.axis_size("block")
    return lax.ppermute(x, "block", [(i, (i + (1 if i % 2 else -1)) % size) for i in range(size)])


def crossed(x, mask):
    return lax.ppermute(x, "block", [(i, i ^ mask) for i in range(lax.axis_size("block"))])


def swapped(x):
    return lax.ppermute(x, "zone", [(i, i ^ 1) for i in range(lax.axis_size("zone"))])


def gather_pair(strip, first):
    x = strip[None]
    bit, size = 1, lax.axis_size("block")
    while 2**bit < size:
        wide = 4 if 2 ** (bit + 1) < size else 2
        pieces = [x] + [crossed(x, k << bit) for k in range(1, wide)]
        *pieces, _ = lax.optimization_barrier((*pieces, first))
        x = jnp.concatenate(pieces, axis=0)
        bit += 2 if wide == 4 else 1
    y = swapped(x)
    return x, y, crossed(x, 1), crossed(y, 1)


def local(
    start_state,
    diffusivity,
    donor_map,
    donor_weight,
    coupling,
    final_cotangent,
    wall_area,
    wall_projection,
    center_ids,
    center_dist,
):
    devices = lax.axis_size("zone") * lax.axis_size("block")
    strip, near, far = pack(
        start_state, final_cotangent, diffusivity, donor_map, donor_weight
    )
    near, far = crossed(near, 1), beyond(far)
    points = wall_gradient(
        start_state, final_cotangent, diffusivity, near, far, coupling, wall_projection,
        wall_area, center_ids, center_dist, devices,
    )
    strips = gather_pair(strip, points)
    points = lax.all_to_all(points, ("zone", "block"), 0, 0, tiled=True)

    adjoint = field(start_state, final_cotangent, diffusivity, near, far, strips, coupling)
    adjoint, points = lax.optimization_barrier((adjoint, points))
    return adjoint, sum_points(points)


def solution(mesh):
    return jax.shard_map(
        local,
        mesh=mesh,
        in_specs=(
            P(None, "zone", "block", None),
            P("zone", "block", None),
            P(None, "zone", None),
            P(None, "zone", None),
            P(),
            P(None, "zone", "block", None),
            P("zone", "block"),
            P(),
            P("zone", None, "block"),
            P("zone", None, "block"),
        ),
        out_specs=(P(None, "zone", "block", None), P(None, ("zone", "block"))),
        check_vma=False,
    )
```

```python
import functools

import jax
import jax.numpy as jnp
from jax import lax
from jax.experimental import pallas as pl
from jax.experimental.pallas import tpu as pltpu
from jax.sharding import PartitionSpec as P

CP_DEV = 256
LANES = 128
SUB = 8
STEPS = 4
NV = 5
UCOLS = STEPS + 2
LCOLS = STEPS
HALO = SUB
ROW_K = 2 * STEPS
ROW_U = ROW_K + UCOLS
ROW_L = ROW_U + NV * UCOLS
STRIP = ROW_L + NV * LCOLS
EDGE_L = NV * UCOLS
EDGE_K = EDGE_L + NV * LCOLS
EDGE = EDGE_K + UCOLS
TAPS = 6
VMEM_LIMIT = 48 * 1024 * 1024


def params(limit=VMEM_LIMIT):
    return pltpu.CompilerParams(vmem_limit_bytes=limit)


def pack_kernel(
    u_hbm, l_hbm, k_hbm, map_hbm, weight_hbm, strip, near, far,
    u_side, l_side, k_side, u_edge, l_edge, k_edge, dmap, dweight, near_offset, sems,
):
    rows, radial = u_hbm.shape[2], u_hbm.shape[3]
    block = lax.axis_index("block")
    own = pl.ds(pl.multiple_of(block * rows, LANES), rows)
    copies = [
        pltpu.make_async_copy(map_hbm.at[:, 0], dmap, sems.at[0, 0]),
        pltpu.make_async_copy(weight_hbm.at[:, 0, own], dweight, sems.at[0, 1]),
    ]
    lanes = pl.ds(radial - LANES, LANES)
    copies += [
        pltpu.make_async_copy(u_hbm.at[:, 0, :, lanes], u_side, sems.at[1, 0]),
        pltpu.make_async_copy(l_hbm.at[:, 0, :, lanes], l_side, sems.at[2, 0]),
        pltpu.make_async_copy(k_hbm.at[0, :, lanes], k_side, sems.at[3, 0]),
    ]
    lower = block % 2 == 0
    top = jnp.where(lower, rows - SUB, 0)
    for i, start in enumerate((top, rows - SUB - top)):
        some = pl.ds(pl.multiple_of(start, SUB), SUB)
        copies += [
            pltpu.make_async_copy(u_hbm.at[:, 0, some], u_edge.at[i], sems.at[4, i]),
            pltpu.make_async_copy(l_hbm.at[:, 0, some], l_edge.at[i], sems.at[5, i]),
            pltpu.make_async_copy(k_hbm.at[0, some], k_edge.at[i], sems.at[6, i]),
        ]
    for copy in copies:
        copy.start()
    for copy in copies:
        copy.wait()
    size = dmap.shape[1]
    delta = dmap[...] - iota(dmap.shape, 1)
    delta = jnp.where(delta < 0, delta + size, delta)
    ahead = delta - delta[:, 0:1] + STEPS
    ahead = jnp.where(ahead < 0, ahead + size, ahead)
    ahead = jnp.where(ahead >= size, ahead - size, ahead).astype(jnp.float32)
    least = jnp.min(ahead, axis=1, keepdims=True)
    offset = delta[:, 0:1].astype(jnp.float32) - float(STEPS) + least
    offset = jnp.where(offset < 0.0, offset + float(size), offset)
    offset = jnp.where(offset >= float(size), offset - float(size), offset)
    near_offset[...] = ahead - least
    strip[0:STEPS, :] = near_offset[:, own]
    which = iota((STEPS, rows), 1) == iota((STEPS, rows), 0)
    offsets = jnp.sum(jnp.where(which, offset, 0.0), axis=0, keepdims=True)
    strip[STEPS : 2 * STEPS, :] = dweight[...]
    strip[ROW_K : ROW_K + 1, :] = offsets
    strip[ROW_K + 1 : ROW_K + UCOLS, :] = k_side[...].T[LANES - UCOLS + 1 :]
    for v in range(NV):
        a, b = ROW_U + v * UCOLS, ROW_L + v * LCOLS
        strip[a : a + UCOLS, :] = u_side[v].T[LANES - UCOLS :]
        strip[b : b + LCOLS, :] = l_side[v].T[LANES - LCOLS :]
    for i, ref in enumerate((near, far)):
        last = lower if i == 0 else jnp.logical_not(lower)

        def ends(x, count):
            return jnp.where(last, x[SUB - count :], x[:count])

        for v in range(NV):
            ref[v * UCOLS : (v + 1) * UCOLS, :] = ends(u_edge[i, v], UCOLS)
            ref[EDGE_L + v * LCOLS : EDGE_L + (v + 1) * LCOLS, :] = ends(l_edge[i, v], LCOLS)
        ref[EDGE_K:EDGE, :] = ends(k_edge[i], UCOLS)


def pack(start_state, final_cotangent, diffusivity, donor_map, donor_weight):
    _, _, rows, radial = start_state.shape
    f32 = jnp.float32
    outs = ((STRIP, rows), (EDGE, radial), (EDGE, radial))
    return pl.pallas_call(
        pack_kernel,
        in_specs=[pl.BlockSpec(memory_space=pltpu.HBM)] * 5,
        out_specs=[pl.BlockSpec(memory_space=pltpu.VMEM)] * 3,
        out_shape=[jax.ShapeDtypeStruct(s, f32) for s in outs],
        scratch_shapes=[
            pltpu.VMEM((NV, rows, LANES), f32),
            pltpu.VMEM((NV, rows, LANES), f32),
            pltpu.VMEM((rows, LANES), f32),
            pltpu.VMEM((2, NV, SUB, radial), f32),
            pltpu.VMEM((2, NV, SUB, radial), f32),
            pltpu.VMEM((2, SUB, radial), f32),
            pltpu.VMEM((STEPS, donor_map.shape[2]), jnp.int32),
            pltpu.VMEM((STEPS, rows), f32),
            pltpu.VMEM((STEPS, donor_map.shape[2]), f32),
            pltpu.SemaphoreType.DMA((7, 2)),
        ],
        compiler_params=params(),
        name="pack",
    )(
        *(
            pltpu.with_memory_space_constraint(x, pltpu.HBM)
            for x in (start_state, final_cotangent, diffusivity, donor_map, donor_weight)
        )
    )


def iota(shape, axis):
    return lax.broadcasted_iota(jnp.int32, shape, axis)


def left(x, by=1):
    return pltpu.roll(x, x.shape[-1] - by, x.ndim - 1)


def right(x, by=1):
    return pltpu.roll(x, by, x.ndim - 1)


def stencil(x):
    inn = jnp.where(iota(x.shape, 0) == 0, 0.0, pltpu.roll(x, 1, 0))
    return left(x) + right(x) + pltpu.roll(x, SUB - 1, 0) + inn - 4.0 * x


def strip_forward(u, t, kappa, c):
    new = []
    for v in range(NV):
        reaction = sum(c[v, w] * t[w] for w in range(NV))
        new.append(u[v] + kappa * stencil(u[v]) - reaction)
    return new


def strip_backward(lam, t, kappa, c):
    new = []
    for v in range(NV):
        pulled = sum(c[w, v] * lam[w] for w in range(NV))
        new.append(lam[v] + stencil(kappa * lam[v]) - (1.0 - t[v] * t[v]) * pulled)
    return new


def wall_kernel(
    u_own, l_own, k_own, near, far, c_ref, proj_ref, area, ids, dist, out, *, devices
):
    rows, nodes = u_own.shape[2], area.shape[1]
    c = {(v, w): c_ref[v : v + 1, w : w + 1] for v in range(NV) for w in range(NV)}
    proj = {(i, v): proj_ref[i : i + 1, v : v + 1] for i in range(3) for v in range(NV)}
    lower = lax.axis_index("block") % 2 == 0
    x, y = near[:, 0:LANES], far[:, 0:LANES]
    gap = jnp.zeros((LANES - 2 * EDGE, LANES), jnp.float32)
    halos = jnp.concatenate([jnp.where(lower, y, x), jnp.where(lower, x, y), gap], axis=0).T[:SUB]
    lane = iota((SUB, LANES), 1)

    def first(own, edge, cols):
        after = pltpu.roll(halos, (LANES - EDGE - edge) % LANES, 1)
        before = pltpu.roll(halos, (LANES - cols - edge) % LANES, 1)
        beside = jnp.where(lane < cols, after, jnp.where(lane >= LANES - cols, before, 0.0))
        return jnp.concatenate([own[:, :LANES].T[:SUB], beside], axis=1)

    kappa = first(k_own.at[0], EDGE_K, UCOLS)
    u = [first(u_own.at[v, 0], v * UCOLS, UCOLS) for v in range(NV)]
    lam = [first(l_own.at[v, 0], EDGE_L + v * LCOLS, LCOLS) for v in range(NV)]
    history = []
    for n in range(STEPS):
        t = [jnp.tanh(x) for x in u]
        history.append((u, t))
        if n < STEPS - 1:
            u = strip_forward(u, t, kappa, c)
    h = [0.0] * NV
    for n in reversed(range(STEPS)):
        u, t = history[n]
        h = [h[v] + (lam[v] * u[v])[0:1, :rows] for v in range(NV)]
        if n > 0:
            lam = strip_backward(lam, t, kappa, c)
    per_row = nodes // rows
    groups = CP_DEV // LANES
    components = [sum(proj[i, v] * h[v] for v in range(NV)) for i in range(3)]
    components += [jnp.zeros((SUB // groups - 3, rows), jnp.float32)]
    s_rows = components * groups
    spread = (iota((rows, nodes), 1) // per_row == iota((rows, nodes), 0)).astype(jnp.float32)
    s = jnp.dot(
        jnp.concatenate(s_rows, axis=0), spread,
        precision=lax.Precision.HIGHEST, preferred_element_type=jnp.float32,
    )
    s = s * area[...]
    d = dist[0]
    q = 1.0 - d
    q = q * q
    phi = q * q * (4.0 * d + 1.0)
    key = ids[0]
    major, minor = key // LANES, key % LANES
    shape = (devices, SUB, nodes)
    target = iota(shape, 0) * groups + iota(shape, 1) // (SUB // groups)
    total = jnp.zeros((devices * SUB, LANES), jnp.float32)
    bf = jnp.bfloat16
    for k in range(d.shape[0]):
        lo = (iota((LANES, nodes), 0) == minor[k : k + 1]).astype(bf)
        hit = target == major[k : k + 1][None]
        w = s * phi[k : k + 1]
        for piece in range(2):
            part = w.astype(bf).astype(jnp.float32)
            w = w - part
            a = jnp.where(hit, part[None], 0.0).reshape(devices * SUB, nodes).astype(bf)
            total += lax.dot_general(
                a, lo, (((1,), (1,)), ((), ())), preferred_element_type=jnp.float32
            )
    total = total.reshape(devices, SUB, LANES)
    for g in range(groups):
        start = g * (SUB // groups)
        out[:, :, g * LANES : (g + 1) * LANES] = total[:, start : start + 3]


def wall_gradient(u, lam, kappa, near, far, coupling, proj, area, ids, dist, devices):
    vm = pl.BlockSpec(memory_space=pltpu.VMEM)
    return pl.pallas_call(
        functools.partial(wall_kernel, devices=devices),
        in_specs=[vm] * 10,
        out_specs=vm,
        out_shape=jax.ShapeDtypeStruct((devices, 3, CP_DEV), jnp.float32),
        compiler_params=params(),
        name="wall_gradient",
    )(u, lam, kappa, near, far, coupling, proj, area, ids, dist)


def face_terms(same, other, c, out, buf, turned, flip, rows, ready):
    block = lax.axis_index("block")
    blocks = 2 * same[0].shape[0]
    shape = (blocks, LANES)
    for m in range(blocks // 2):
        at = block ^ (2 * m)
        for q in range(2):
            start = q * STRIP * blocks
            buf[pl.ds(start + at, STRIP, stride=blocks), :] = same[q][m]
            buf[pl.ds(start + (at ^ 1), STRIP, stride=blocks), :] = other[q][m]

    def load(q, row):
        return buf[pl.ds((q * STRIP + row) * blocks, blocks), :]

    lane = iota(shape, 1)

    def later(x, by=1):
        y = jnp.where(lane >= by, x, pltpu.roll(x, blocks - 1, 0))
        return pltpu.roll(y, LANES - by, 1)

    def earlier(x, by=1):
        y = jnp.where(lane < LANES - by, x, pltpu.roll(x, 1, 0))
        return pltpu.roll(y, by, 1)

    far, taps = {}, {}
    for q in range(2):
        for n in range(STEPS):
            t = load(q, ROW_K)[0:1, n : n + 1].astype(jnp.int32)[0, 0]
            far[q, n] = (t // LANES, t % LANES)
            e = load(q, n)
            share = load(q, STEPS + n)
            taps[q, n] = [
                jnp.where(e == float(i), share, 0.0)
                + jnp.where(e == float(i - 1), 1.0 - share, 0.0)
                for i in range(TAPS)
            ]

    def shifts(q, n):
        whole, rest = far[q, n]
        return whole, [
            (jnp.where(rest + i < LANES, rest + i, rest + i - LANES), lane >= rest + i,
             lane >= rest + i - LANES)
            for i in range(TAPS)
        ]

    def ghost(q, n, faces):
        whole, moves = shifts(q, n)
        result = []
        for f in faces:
            near = [pltpu.roll(f, (2 * blocks - whole - k) % blocks, 0) for k in range(3)]
            acc = 0.0
            for i, (by, here, next_one) in enumerate(moves):
                y = jnp.where(here, near[0], jnp.where(next_one, near[1], near[2]))
                acc = acc + taps[q, n][i] * pltpu.roll(y, (LANES - by) % LANES, 1)
            result.append(acc)
        return result

    def back(q, n, faces):
        whole, moves = shifts(q, n)
        result = []
        for f in faces:
            parts = [0.0, 0.0, 0.0]
            for i, (by, here, next_one) in enumerate(moves):
                y = pltpu.roll(taps[q, n][i] * f, by, 1)
                parts[0] = parts[0] + jnp.where(here, y, 0.0)
                parts[1] = parts[1] + jnp.where(here, 0.0, jnp.where(next_one, y, 0.0))
                parts[2] = parts[2] + jnp.where(next_one, 0.0, y)
            result.append(
                sum(pltpu.roll(parts[k], (whole + k) % blocks, 0) for k in range(3))
            )
        return result

    def emit(index, g):
        for v in range(NV):
            turned[pl.ds((index * SUB + v) * blocks, blocks), :] = g[v]

    last = UCOLS - 1
    kappa = [[load(q, ROW_K + k) for k in range(UCOLS)] for q in range(2)]
    u = [
        [{k: load(q, ROW_U + v * UCOLS + k) for k in range(UCOLS)} for v in range(NV)]
        for q in range(2)
    ]
    gap = UCOLS - LCOLS
    lam = [
        [{k: load(q, ROW_L + v * LCOLS + k - gap) for k in range(gap, UCOLS)} for v in range(NV)]
        for q in range(2)
    ]
    history = {}
    ready()
    for n in range(STEPS):
        first = n + 1 if n < STEPS - 1 else STEPS - 1
        for q in range(2):
            history[n, q] = [
                {k: jnp.tanh(u[q][v][k]) for k in range(first, UCOLS)} for v in range(NV)
            ]
        if n == STEPS - 1:
            break
        g = [ghost(q, n, [u[1 - q][v][last] for v in range(NV)]) for q in range(2)]
        emit(n, g[0])
        new = []
        for q in range(2):
            side = []
            for v in range(NV):
                cols = {}
                for k in range(n + 1, UCOLS):
                    x = u[q][v][k]
                    outer = u[q][v][k + 1] if k < last else g[q][v]
                    lap = later(x) + earlier(x) + u[q][v][k - 1] + outer - 4.0 * x
                    reaction = sum(c[v, w] * history[n, q][w][k] for w in range(NV))
                    cols[k] = x + kappa[q][k] * lap - reaction
                side.append(cols)
            new.append(side)
        u = new
    for n in reversed(range(STEPS)):
        s = [
            [{k: kappa[q][k] * x for k, x in lam[q][v].items()} for v in range(NV)]
            for q in range(2)
        ]
        sides = (0, 1) if n > 1 else (1,) if n == 1 else ()
        g = {
            q: back(1 - q, n, [s[1 - q][v][last] for v in range(NV)]) for q in {0, *sides}
        }
        emit(STEPS - 1 + n, g[0])
        new = [None, None]
        for q in sides:
            side = []
            for v in range(NV):
                cols = {}
                for k in range(UCOLS - n, UCOLS):
                    x = lam[q][v][k]
                    y = s[q][v][k]
                    outer = s[q][v][k + 1] if k < last else g[q][v]
                    lap = later(y) + earlier(y) + s[q][v][k - 1] + outer - 4.0 * y
                    pulled = sum(c[w, v] * lam[q][w][k] for w in range(NV))
                    t = history[n, q][v][k]
                    cols[k] = x + lap - (1.0 - t * t) * pulled
                side.append(cols)
            new[q] = side
        if n == 1:
            new[0] = [{last: jnp.zeros(shape, jnp.float32)} for v in range(NV)]
        lam = new

    count = (2 * STEPS - 1) * SUB
    flip[...] = jnp.zeros_like(flip)
    around = [
        turned[pl.ds(lax.rem(block + shift + blocks, blocks), count, stride=blocks), :]
        for shift in (-1, 0, 1)
    ]
    wide = jnp.concatenate(around, axis=1)
    wide = pltpu.roll(wide, wide.shape[1] - (LANES - HALO), 1)
    flip[0:count, :] = wide[:, : 2 * LANES]
    for j in range(2):
        out[j * LANES : (j + 1) * LANES, :] = flip[:, j * LANES : (j + 1) * LANES].T


def field_kernel(
    u_hbm, l_hbm, k_hbm, near, far, same_0, same_1, other_0, other_1, c_hbm, out,
    c, ext_u, ext_l, ext_k, kap, rest, states, tanhs, lam, scaled, terms, buf, turned, flip, sems,
):
    rows, radial = u_hbm.shape[2], u_hbm.shape[3]
    chunks = kap.shape[0]
    tiles = radial // LANES
    own = pl.ds(HALO, rows)

    def cut(j):
        return slice(j * LANES, (j + 1) * LANES)

    c_copy = pltpu.make_async_copy(c_hbm, c, sems.at[4, 0])
    c_copy.start()
    copies = []
    for j in range(tiles):
        lanes = pl.ds(j * LANES, LANES)
        copies += [
            pltpu.make_async_copy(u_hbm.at[:, 0, :, lanes], ext_u.at[:, j, own], sems.at[0, j]),
            pltpu.make_async_copy(l_hbm.at[:, 0, :, lanes], ext_l.at[:, j, own], sems.at[1, j]),
            pltpu.make_async_copy(k_hbm.at[0, :, lanes], ext_k.at[j, own], sems.at[2, j]),
        ]
    for copy in copies:
        copy.start()
    face_terms(
        (same_0, same_1), (other_0, other_1), c, terms, buf, turned, flip, rows, c_copy.wait
    )
    lower = lax.axis_index("block") % 2 == 0

    def halo(a, b, cols):
        x, y = near[a:b, cols], far[a:b, cols]
        return jnp.where(lower, y, x), jnp.where(lower, x, y)

    def put(ref, where, pair, count):
        gap = jnp.zeros((HALO - count, LANES), jnp.float32)
        ref[(*where, pl.ds(0, HALO))] = jnp.concatenate([gap, pair[0]], axis=0)
        ref[(*where, pl.ds(HALO + rows, HALO))] = jnp.concatenate([pair[1], gap], axis=0)

    for j in range(tiles):
        put(ext_k, (j,), halo(EDGE_K, EDGE, cut(j)), UCOLS)
        for v in range(NV):
            put(ext_u, (v, j), halo(v * UCOLS, (v + 1) * UCOLS, cut(j)), UCOLS)
            at = EDGE_L + v * LCOLS
            put(ext_l, (v, j), halo(at, at + LCOLS, cut(j)), LCOLS)
    for copy in copies:
        copy.wait()

    def load(i, carry):
        at = pl.ds(i, SUB, stride=chunks)
        for j in range(tiles):
            kappa = ext_k[j, at, :]
            kap[i, :, cut(j)] = kappa
            rest[i, :, cut(j)] = 1.0 - 4.0 * kappa
            for v in range(NV):
                states[0, v, i + 1, :, cut(j)] = ext_u[v, j, at, :]
                x = ext_l[v, j, at, :]
                lam[v, i, :, cut(j)] = x
                scaled[0, v, i + 1, :, cut(j)] = kappa * x
        return carry

    lax.fori_loop(0, chunks, load, 0, unroll=2)

    def wrap(ref):
        for v in range(NV):
            ref[v, 0] = pltpu.roll(ref[v, chunks], 1, 0)
            ref[v, chunks + 1] = pltpu.roll(ref[v, 1], SUB - 1, 0)

    wrap(states.at[0])
    wrap(scaled.at[0])
    lane = iota((SUB, LANES), 1)
    is_first, is_last = lane == 0, lane == LANES - 1

    def neighbours(ref, v, i, j, edge, cache):
        def tile(b):
            if (v, b) not in cache:
                x = ref[v, i + 1, :, cut(b)]
                cache[v, b] = (x, pltpu.roll(x, 1, 1), pltpu.roll(x, LANES - 1, 1))
            return cache[v, b]

        x, r, l = tile(j)
        inn = jnp.where(is_first, tile(j - 1)[1] if j > 0 else 0.0, r)
        outv = jnp.where(is_last, tile(j + 1)[2] if j < tiles - 1 else edge, l)
        return ref[v, i, :, cut(j)] + ref[v, i + 2, :, cut(j)] + inn + outv, x

    def edges(i, n):
        e = terms[pl.ds(i, SUB, stride=chunks), :]
        return [pltpu.roll(e, (2 * LANES - 1 - (n * SUB + v)) % LANES, 1) for v in range(NV)]

    def forward(n):
        def body(i, carry):
            edge = edges(i, n)
            cache = {}
            for j in range(tiles):
                kappa = kap[i, :, cut(j)]
                pairs = [neighbours(states.at[n], v, i, j, edge[v], cache) for v in range(NV)]
                t = [jnp.tanh(x) for _, x in pairs]
                for v in range(NV):
                    around, x = pairs[v]
                    tanhs[n, v, i, :, cut(j)] = t[v]
                    reaction = sum(c[v, w] * t[w] for w in range(NV))
                    states[n + 1, v, i + 1, :, cut(j)] = (
                        rest[i, :, cut(j)] * x + kappa * around - reaction
                    )
            return carry

        lax.fori_loop(0, chunks, body, 0, unroll=chunks)
        if n + 1 < STEPS - 1:
            wrap(states.at[n + 1])

    def backward(n, source, target, chosen):
        def body(i, carry):
            edge = edges(i, STEPS - 1 + n)
            cache = {}
            for j in range(tiles):
                kappa = kap[i, :, cut(j)]
                x = [lam[v, i, :, cut(j)] for v in range(NV)]
                for v in chosen:
                    around, _ = neighbours(scaled.at[source], v, i, j, edge[v], cache)
                    if n < STEPS - 1:
                        t = tanhs[n, v, i, :, cut(j)]
                    else:
                        t = jnp.tanh(states[n, v, i + 1, :, cut(j)])
                    pulled = sum(c[w, v] * x[w] for w in range(NV))
                    new = rest[i, :, cut(j)] * x[v] + around - (1.0 - t * t) * pulled
                    if n > 0:
                        lam[v, i, :, cut(j)] = new
                        scaled[target, v, i + 1, :, cut(j)] = kappa * new
                    else:
                        ext_l[v, j, pl.ds(i, SUB, stride=chunks), :] = new
            return carry

        lax.fori_loop(0, chunks, body, 0, unroll=chunks)
        if n > 0:
            wrap(scaled.at[target])

    for n in range(STEPS - 1):
        forward(n)
    source = 0
    for n in reversed(range(1, STEPS)):
        backward(n, source, 1 - source, range(NV))
        source = 1 - source
    copies = []
    for v in range(NV):
        backward(0, source, 1 - source, (v,))
        for j in range(tiles):
            lanes = pl.ds(j * LANES, LANES)
            copies.append(
                pltpu.make_async_copy(
                    ext_l.at[v, j, own], out.at[v, 0, :, lanes], sems.at[5 + v, j]
                )
            )
            copies[-1].start()
    for copy in copies:
        copy.wait()


def field(start_state, final_cotangent, diffusivity, near, far, strips, coupling):
    _, _, rows, radial = start_state.shape
    ext = rows + 2 * HALO
    chunks, tiles, blocks = ext // SUB, radial // LANES, 2 * strips[0].shape[0]
    vm = pl.BlockSpec(memory_space=pltpu.VMEM)
    hbm = pl.BlockSpec(memory_space=pltpu.HBM)
    f32 = jnp.float32
    return pl.pallas_call(
        field_kernel,
        in_specs=[vm] * 9 + [hbm],
        out_specs=hbm,
        out_shape=jax.ShapeDtypeStruct(start_state.shape, f32),
        scratch_shapes=[
            pltpu.SMEM(coupling.shape, f32),
            pltpu.VMEM((NV, tiles, ext, LANES), f32),
            pltpu.VMEM((NV, tiles, ext, LANES), f32),
            pltpu.VMEM((tiles, ext, LANES), f32),
            pltpu.VMEM((chunks, SUB, radial), f32),
            pltpu.VMEM((chunks, SUB, radial), f32),
            pltpu.VMEM((STEPS, NV, chunks + 2, SUB, radial), f32),
            pltpu.VMEM((STEPS - 1, NV, chunks, SUB, radial), f32),
            pltpu.VMEM((NV, chunks, SUB, radial), f32),
            pltpu.VMEM((2, NV, chunks + 2, SUB, radial), f32),
            pltpu.VMEM((2 * LANES, LANES), f32),
            pltpu.VMEM((2 * STRIP * blocks, LANES), f32),
            pltpu.VMEM(((2 * STEPS - 1) * SUB * blocks, LANES), f32),
            pltpu.VMEM((LANES, 2 * LANES), f32),
            pltpu.SemaphoreType.DMA((5 + NV, tiles)),
        ],
        compiler_params=params(),
        name="field",
    )(start_state, final_cotangent, diffusivity, near, far, *strips, coupling)


def beyond(x):
    size = lax.axis_size("block")
    return lax.ppermute(x, "block", [(i, (i + (1 if i % 2 else -1)) % size) for i in range(size)])


def crossed(x, mask):
    return lax.ppermute(x, "block", [(i, i ^ mask) for i in range(lax.axis_size("block"))])


def swapped(x):
    return lax.ppermute(x, "zone", [(i, i ^ 1) for i in range(lax.axis_size("zone"))])


def gather_pair(strip, first):
    x = strip[None]
    bit, size = 1, lax.axis_size("block")
    while 2**bit < size:
        wide = 4 if 2 ** (bit + 1) < size else 2
        pieces = [x] + [crossed(x, k << bit) for k in range(1, wide)]
        *pieces, _ = lax.optimization_barrier((*pieces, first))
        x = jnp.concatenate(pieces, axis=0)
        bit += 2 if wide == 4 else 1
    y = swapped(x)
    return x, y, crossed(x, 1), crossed(y, 1)


def local(
    start_state,
    diffusivity,
    donor_map,
    donor_weight,
    coupling,
    final_cotangent,
    wall_area,
    wall_projection,
    center_ids,
    center_dist,
):
    devices = lax.axis_size("zone") * lax.axis_size("block")
    strip, near, far = pack(
        start_state, final_cotangent, diffusivity, donor_map, donor_weight
    )
    near, far = crossed(near, 1), beyond(far)
    points = wall_gradient(
        start_state, final_cotangent, diffusivity, near, far, coupling, wall_projection,
        wall_area, center_ids, center_dist, devices,
    )
    strips = gather_pair(strip, points)
    points = lax.all_to_all(points, ("zone", "block"), 0, 0, tiled=True)

    adjoint = field(start_state, final_cotangent, diffusivity, near, far, strips, coupling)
    adjoint, points = lax.optimization_barrier((adjoint, points))
    return adjoint, points.sum(axis=0)


def solution(mesh):
    return jax.shard_map(
        local,
        mesh=mesh,
        in_specs=(
            P(None, "zone", "block", None),
            P("zone", "block", None),
            P(None, "zone", None),
            P(None, "zone", None),
            P(),
            P(None, "zone", "block", None),
            P("zone", "block"),
            P(),
            P("zone", None, "block"),
            P("zone", None, "block"),
        ),
        out_specs=(P(None, "zone", "block", None), P(None, ("zone", "block"))),
        check_vma=False,
    )
```

```python
import functools

import jax
import jax.numpy as jnp
from jax import lax
from jax.experimental import pallas as pl
from jax.experimental.pallas import tpu as pltpu
from jax.sharding import PartitionSpec as P

CP_DEV = 256
LANES = 128
SUB = 8
STEPS = 4
NV = 5
UCOLS = STEPS + 2
LCOLS = STEPS
HALO = SUB
ROW_K = 2 * STEPS
ROW_U = ROW_K + UCOLS
ROW_L = ROW_U + NV * UCOLS
STRIP = ROW_L + NV * LCOLS
EDGE_L = NV * UCOLS
EDGE_K = EDGE_L + NV * LCOLS
EDGE = EDGE_K + UCOLS
TAPS = 6
VMEM_LIMIT = 48 * 1024 * 1024


def params(limit=VMEM_LIMIT):
    return pltpu.CompilerParams(vmem_limit_bytes=limit)


def pack_kernel(
    u_hbm, l_hbm, k_hbm, map_hbm, weight_hbm, strip, near, far,
    u_side, l_side, k_side, u_edge, l_edge, k_edge, dmap, dweight, near_offset, sems,
):
    rows, radial = u_hbm.shape[2], u_hbm.shape[3]
    block = lax.axis_index("block")
    own = pl.ds(pl.multiple_of(block * rows, LANES), rows)
    copies = [
        pltpu.make_async_copy(map_hbm.at[:, 0], dmap, sems.at[0, 0]),
        pltpu.make_async_copy(weight_hbm.at[:, 0, own], dweight, sems.at[0, 1]),
    ]
    lanes = pl.ds(radial - LANES, LANES)
    copies += [
        pltpu.make_async_copy(u_hbm.at[:, 0, :, lanes], u_side, sems.at[1, 0]),
        pltpu.make_async_copy(l_hbm.at[:, 0, :, lanes], l_side, sems.at[2, 0]),
        pltpu.make_async_copy(k_hbm.at[0, :, lanes], k_side, sems.at[3, 0]),
    ]
    lower = block % 2 == 0
    top = jnp.where(lower, rows - SUB, 0)
    for i, start in enumerate((top, rows - SUB - top)):
        some = pl.ds(pl.multiple_of(start, SUB), SUB)
        copies += [
            pltpu.make_async_copy(u_hbm.at[:, 0, some], u_edge.at[i], sems.at[4, i]),
            pltpu.make_async_copy(l_hbm.at[:, 0, some], l_edge.at[i], sems.at[5, i]),
            pltpu.make_async_copy(k_hbm.at[0, some], k_edge.at[i], sems.at[6, i]),
        ]
    for copy in copies:
        copy.start()
    for copy in copies[:2]:
        copy.wait()
    size = dmap.shape[1]
    delta = dmap[...] - iota(dmap.shape, 1)
    delta = jnp.where(delta < 0, delta + size, delta)
    ahead = delta - delta[:, 0:1] + STEPS
    ahead = jnp.where(ahead < 0, ahead + size, ahead)
    ahead = jnp.where(ahead >= size, ahead - size, ahead).astype(jnp.float32)
    least = jnp.min(ahead, axis=1, keepdims=True)
    offset = delta[:, 0:1].astype(jnp.float32) - float(STEPS) + least
    offset = jnp.where(offset < 0.0, offset + float(size), offset)
    offset = jnp.where(offset >= float(size), offset - float(size), offset)
    near_offset[...] = ahead - least
    strip[0:STEPS, :] = near_offset[:, own]
    which = iota((STEPS, rows), 1) == iota((STEPS, rows), 0)
    offsets = jnp.sum(jnp.where(which, offset, 0.0), axis=0, keepdims=True)
    strip[STEPS : 2 * STEPS, :] = dweight[...]
    for copy in copies[2:5]:
        copy.wait()
    strip[ROW_K : ROW_K + 1, :] = offsets
    strip[ROW_K + 1 : ROW_K + UCOLS, :] = k_side[...].T[LANES - UCOLS + 1 :]
    for v in range(NV):
        a, b = ROW_U + v * UCOLS, ROW_L + v * LCOLS
        strip[a : a + UCOLS, :] = u_side[v].T[LANES - UCOLS :]
        strip[b : b + LCOLS, :] = l_side[v].T[LANES - LCOLS :]
    for copy in copies[5:]:
        copy.wait()
    for i, ref in enumerate((near, far)):
        last = lower if i == 0 else jnp.logical_not(lower)

        def ends(x, count):
            return jnp.where(last, x[SUB - count :], x[:count])

        for v in range(NV):
            ref[v * UCOLS : (v + 1) * UCOLS, :] = ends(u_edge[i, v], UCOLS)
            ref[EDGE_L + v * LCOLS : EDGE_L + (v + 1) * LCOLS, :] = ends(l_edge[i, v], LCOLS)
        ref[EDGE_K:EDGE, :] = ends(k_edge[i], UCOLS)


def pack(start_state, final_cotangent, diffusivity, donor_map, donor_weight):
    _, _, rows, radial = start_state.shape
    f32 = jnp.float32
    outs = ((STRIP, rows), (EDGE, radial), (EDGE, radial))
    return pl.pallas_call(
        pack_kernel,
        in_specs=[pl.BlockSpec(memory_space=pltpu.HBM)] * 5,
        out_specs=[pl.BlockSpec(memory_space=pltpu.VMEM)] * 3,
        out_shape=[jax.ShapeDtypeStruct(s, f32) for s in outs],
        scratch_shapes=[
            pltpu.VMEM((NV, rows, LANES), f32),
            pltpu.VMEM((NV, rows, LANES), f32),
            pltpu.VMEM((rows, LANES), f32),
            pltpu.VMEM((2, NV, SUB, radial), f32),
            pltpu.VMEM((2, NV, SUB, radial), f32),
            pltpu.VMEM((2, SUB, radial), f32),
            pltpu.VMEM((STEPS, donor_map.shape[2]), jnp.int32),
            pltpu.VMEM((STEPS, rows), f32),
            pltpu.VMEM((STEPS, donor_map.shape[2]), f32),
            pltpu.SemaphoreType.DMA((7, 2)),
        ],
        compiler_params=params(),
        name="pack",
    )(
        *(
            pltpu.with_memory_space_constraint(x, pltpu.HBM)
            for x in (start_state, final_cotangent, diffusivity, donor_map, donor_weight)
        )
    )


def iota(shape, axis):
    return lax.broadcasted_iota(jnp.int32, shape, axis)


def left(x, by=1):
    return pltpu.roll(x, x.shape[-1] - by, x.ndim - 1)


def right(x, by=1):
    return pltpu.roll(x, by, x.ndim - 1)


def stencil(x):
    inn = jnp.where(iota(x.shape, 0) == 0, 0.0, pltpu.roll(x, 1, 0))
    return left(x) + right(x) + pltpu.roll(x, SUB - 1, 0) + inn - 4.0 * x


def strip_forward(u, t, kappa, c):
    new = []
    for v in range(NV):
        reaction = sum(c[v, w] * t[w] for w in range(NV))
        new.append(u[v] + kappa * stencil(u[v]) - reaction)
    return new


def strip_backward(lam, t, kappa, c):
    new = []
    for v in range(NV):
        pulled = sum(c[w, v] * lam[w] for w in range(NV))
        new.append(lam[v] + stencil(kappa * lam[v]) - (1.0 - t[v] * t[v]) * pulled)
    return new


def wall_kernel(
    u_own, l_own, k_own, near, far, c_ref, proj_ref, area, ids, dist, out, *, devices
):
    rows, nodes = u_own.shape[2], area.shape[1]
    c = {(v, w): c_ref[v : v + 1, w : w + 1] for v in range(NV) for w in range(NV)}
    proj = {(i, v): proj_ref[i : i + 1, v : v + 1] for i in range(3) for v in range(NV)}
    lower = lax.axis_index("block") % 2 == 0
    x, y = near[:, 0:LANES], far[:, 0:LANES]
    gap = jnp.zeros((LANES - 2 * EDGE, LANES), jnp.float32)
    halos = jnp.concatenate([jnp.where(lower, y, x), jnp.where(lower, x, y), gap], axis=0).T[:SUB]
    lane = iota((SUB, LANES), 1)

    def first(own, edge, cols):
        after = pltpu.roll(halos, (LANES - EDGE - edge) % LANES, 1)
        before = pltpu.roll(halos, (LANES - cols - edge) % LANES, 1)
        beside = jnp.where(lane < cols, after, jnp.where(lane >= LANES - cols, before, 0.0))
        return jnp.concatenate([own[:, :LANES].T[:SUB], beside], axis=1)

    kappa = first(k_own.at[0], EDGE_K, UCOLS)
    u = [first(u_own.at[v, 0], v * UCOLS, UCOLS) for v in range(NV)]
    lam = [first(l_own.at[v, 0], EDGE_L + v * LCOLS, LCOLS) for v in range(NV)]
    history = []
    for n in range(STEPS):
        t = [jnp.tanh(x) for x in u]
        history.append((u, t))
        if n < STEPS - 1:
            u = strip_forward(u, t, kappa, c)
    h = [0.0] * NV
    for n in reversed(range(STEPS)):
        u, t = history[n]
        h = [h[v] + (lam[v] * u[v])[0:1, :rows] for v in range(NV)]
        if n > 0:
            lam = strip_backward(lam, t, kappa, c)
    per_row = nodes // rows
    groups = CP_DEV // LANES
    components = [sum(proj[i, v] * h[v] for v in range(NV)) for i in range(3)]
    components += [jnp.zeros((SUB // groups - 3, rows), jnp.float32)]
    s_rows = components * groups
    spread = (iota((rows, nodes), 1) // per_row == iota((rows, nodes), 0)).astype(jnp.float32)
    s = jnp.dot(
        jnp.concatenate(s_rows, axis=0), spread,
        precision=lax.Precision.HIGHEST, preferred_element_type=jnp.float32,
    )
    s = s * area[...]
    d = dist[0]
    q = 1.0 - d
    q = q * q
    phi = q * q * (4.0 * d + 1.0)
    key = ids[0]
    major, minor = key // LANES, key % LANES
    shape = (devices, SUB, nodes)
    target = iota(shape, 0) * groups + iota(shape, 1) // (SUB // groups)
    total = jnp.zeros((devices * SUB, LANES), jnp.float32)
    bf = jnp.bfloat16
    for k in range(d.shape[0]):
        lo = (iota((LANES, nodes), 0) == minor[k : k + 1]).astype(bf)
        hit = target == major[k : k + 1][None]
        w = s * phi[k : k + 1]
        for piece in range(2):
            part = w.astype(bf).astype(jnp.float32)
            w = w - part
            a = jnp.where(hit, part[None], 0.0).reshape(devices * SUB, nodes).astype(bf)
            total += lax.dot_general(
                a, lo, (((1,), (1,)), ((), ())), preferred_element_type=jnp.float32
            )
    total = total.reshape(devices, SUB, LANES)
    for g in range(groups):
        start = g * (SUB // groups)
        out[:, :, g * LANES : (g + 1) * LANES] = total[:, start : start + 3]


def wall_gradient(u, lam, kappa, near, far, coupling, proj, area, ids, dist, devices):
    vm = pl.BlockSpec(memory_space=pltpu.VMEM)
    return pl.pallas_call(
        functools.partial(wall_kernel, devices=devices),
        in_specs=[vm] * 10,
        out_specs=vm,
        out_shape=jax.ShapeDtypeStruct((devices, 3, CP_DEV), jnp.float32),
        compiler_params=params(),
        name="wall_gradient",
    )(u, lam, kappa, near, far, coupling, proj, area, ids, dist)


def face_terms(same, other, c, out, buf, turned, flip, rows, ready):
    block = lax.axis_index("block")
    blocks = 2 * same[0].shape[0]
    shape = (blocks, LANES)
    for m in range(blocks // 2):
        at = block ^ (2 * m)
        for q in range(2):
            start = q * STRIP * blocks
            buf[pl.ds(start + at, STRIP, stride=blocks), :] = same[q][m]
            buf[pl.ds(start + (at ^ 1), STRIP, stride=blocks), :] = other[q][m]

    def load(q, row):
        return buf[pl.ds((q * STRIP + row) * blocks, blocks), :]

    lane = iota(shape, 1)

    def later(x, by=1):
        y = jnp.where(lane >= by, x, pltpu.roll(x, blocks - 1, 0))
        return pltpu.roll(y, LANES - by, 1)

    def earlier(x, by=1):
        y = jnp.where(lane < LANES - by, x, pltpu.roll(x, 1, 0))
        return pltpu.roll(y, by, 1)

    far, taps = {}, {}
    for q in range(2):
        for n in range(STEPS):
            t = load(q, ROW_K)[0:1, n : n + 1].astype(jnp.int32)[0, 0]
            far[q, n] = (t // LANES, t % LANES)
            e = load(q, n)
            share = load(q, STEPS + n)
            taps[q, n] = [
                jnp.where(e == float(i), share, 0.0)
                + jnp.where(e == float(i - 1), 1.0 - share, 0.0)
                for i in range(TAPS)
            ]

    def shifts(q, n):
        whole, rest = far[q, n]
        return whole, [
            (jnp.where(rest + i < LANES, rest + i, rest + i - LANES), lane >= rest + i,
             lane >= rest + i - LANES)
            for i in range(TAPS)
        ]

    def ghost(q, n, faces):
        whole, moves = shifts(q, n)
        result = []
        for f in faces:
            near = [pltpu.roll(f, (2 * blocks - whole - k) % blocks, 0) for k in range(3)]
            acc = 0.0
            for i, (by, here, next_one) in enumerate(moves):
                y = jnp.where(here, near[0], jnp.where(next_one, near[1], near[2]))
                acc = acc + taps[q, n][i] * pltpu.roll(y, (LANES - by) % LANES, 1)
            result.append(acc)
        return result

    def back(q, n, faces):
        whole, moves = shifts(q, n)
        result = []
        for f in faces:
            parts = [0.0, 0.0, 0.0]
            for i, (by, here, next_one) in enumerate(moves):
                y = pltpu.roll(taps[q, n][i] * f, by, 1)
                parts[0] = parts[0] + jnp.where(here, y, 0.0)
                parts[1] = parts[1] + jnp.where(here, 0.0, jnp.where(next_one, y, 0.0))
                parts[2] = parts[2] + jnp.where(next_one, 0.0, y)
            result.append(
                sum(pltpu.roll(parts[k], (whole + k) % blocks, 0) for k in range(3))
            )
        return result

    def emit(index, g):
        for v in range(NV):
            turned[pl.ds((index * SUB + v) * blocks, blocks), :] = g[v]

    last = UCOLS - 1
    kappa = [[load(q, ROW_K + k) for k in range(UCOLS)] for q in range(2)]
    u = [
        [{k: load(q, ROW_U + v * UCOLS + k) for k in range(UCOLS)} for v in range(NV)]
        for q in range(2)
    ]
    gap = UCOLS - LCOLS
    lam = [
        [{k: load(q, ROW_L + v * LCOLS + k - gap) for k in range(gap, UCOLS)} for v in range(NV)]
        for q in range(2)
    ]
    history = {}
    ready()
    for n in range(STEPS):
        first = n + 1 if n < STEPS - 1 else STEPS - 1
        for q in range(2):
            history[n, q] = [
                {k: jnp.tanh(u[q][v][k]) for k in range(first, UCOLS)} for v in range(NV)
            ]
        if n == STEPS - 1:
            break
        g = [ghost(q, n, [u[1 - q][v][last] for v in range(NV)]) for q in range(2)]
        emit(n, g[0])
        new = []
        for q in range(2):
            side = []
            for v in range(NV):
                cols = {}
                for k in range(n + 1, UCOLS):
                    x = u[q][v][k]
                    outer = u[q][v][k + 1] if k < last else g[q][v]
                    lap = later(x) + earlier(x) + u[q][v][k - 1] + outer - 4.0 * x
                    reaction = sum(c[v, w] * history[n, q][w][k] for w in range(NV))
                    cols[k] = x + kappa[q][k] * lap - reaction
                side.append(cols)
            new.append(side)
        u = new
    for n in reversed(range(STEPS)):
        s = [
            [{k: kappa[q][k] * x for k, x in lam[q][v].items()} for v in range(NV)]
            for q in range(2)
        ]
        sides = (0, 1) if n > 1 else (1,) if n == 1 else ()
        g = {
            q: back(1 - q, n, [s[1 - q][v][last] for v in range(NV)]) for q in {0, *sides}
        }
        emit(STEPS - 1 + n, g[0])
        new = [None, None]
        for q in sides:
            side = []
            for v in range(NV):
                cols = {}
                for k in range(UCOLS - n, UCOLS):
                    x = lam[q][v][k]
                    y = s[q][v][k]
                    outer = s[q][v][k + 1] if k < last else g[q][v]
                    lap = later(y) + earlier(y) + s[q][v][k - 1] + outer - 4.0 * y
                    pulled = sum(c[w, v] * lam[q][w][k] for w in range(NV))
                    t = history[n, q][v][k]
                    cols[k] = x + lap - (1.0 - t * t) * pulled
                side.append(cols)
            new[q] = side
        if n == 1:
            new[0] = [{last: jnp.zeros(shape, jnp.float32)} for v in range(NV)]
        lam = new

    count = (2 * STEPS - 1) * SUB
    flip[...] = jnp.zeros_like(flip)
    around = [
        turned[pl.ds(lax.rem(block + shift + blocks, blocks), count, stride=blocks), :]
        for shift in (-1, 0, 1)
    ]
    wide = jnp.concatenate(around, axis=1)
    wide = pltpu.roll(wide, wide.shape[1] - (LANES - HALO), 1)
    flip[0:count, :] = wide[:, : 2 * LANES]
    for j in range(2):
        out[j * LANES : (j + 1) * LANES, :] = flip[:, j * LANES : (j + 1) * LANES].T


def wrap(ref):
    chunks = ref.shape[1] - 2
    for v in range(NV):
        ref[v, 0] = pltpu.roll(ref[v, chunks], 1, 0)
        ref[v, chunks + 1] = pltpu.roll(ref[v, 1], SUB - 1, 0)


def stage_kernel(
    u_own, l_own, k_own, near, far, state, lam, scaled, kap, rest, ext_u, ext_l, ext_k, sems
):
    rows, radial = u_own.shape[2], u_own.shape[3]
    chunks = kap.shape[0]
    tiles = radial // LANES
    own = pl.ds(HALO, rows)

    def cut(j):
        return slice(j * LANES, (j + 1) * LANES)

    copies = []
    for j in range(tiles):
        lanes = pl.ds(j * LANES, LANES)
        copies += [
            pltpu.make_async_copy(u_own.at[:, 0, :, lanes], ext_u.at[:, j, own], sems.at[0, j]),
            pltpu.make_async_copy(l_own.at[:, 0, :, lanes], ext_l.at[:, j, own], sems.at[1, j]),
            pltpu.make_async_copy(k_own.at[0, :, lanes], ext_k.at[j, own], sems.at[2, j]),
        ]
    for copy in copies:
        copy.start()
    lower = lax.axis_index("block") % 2 == 0

    def halo(a, b, cols):
        x, y = near[a:b, cols], far[a:b, cols]
        return jnp.where(lower, y, x), jnp.where(lower, x, y)

    def put(ref, where, pair, count):
        gap = jnp.zeros((HALO - count, LANES), jnp.float32)
        ref[(*where, pl.ds(0, HALO))] = jnp.concatenate([gap, pair[0]], axis=0)
        ref[(*where, pl.ds(HALO + rows, HALO))] = jnp.concatenate([pair[1], gap], axis=0)

    for j in range(tiles):
        put(ext_k, (j,), halo(EDGE_K, EDGE, cut(j)), UCOLS)
        for v in range(NV):
            put(ext_u, (v, j), halo(v * UCOLS, (v + 1) * UCOLS, cut(j)), UCOLS)
            at = EDGE_L + v * LCOLS
            put(ext_l, (v, j), halo(at, at + LCOLS, cut(j)), LCOLS)
    for copy in copies:
        copy.wait()

    def load(i, carry):
        at = pl.ds(i, SUB, stride=chunks)
        for j in range(tiles):
            kappa = ext_k[j, at, :]
            kap[i, :, cut(j)] = kappa
            rest[i, :, cut(j)] = 1.0 - 4.0 * kappa
            for v in range(NV):
                state[v, i + 1, :, cut(j)] = ext_u[v, j, at, :]
                x = ext_l[v, j, at, :]
                lam[v, i, :, cut(j)] = x
                scaled[v, i + 1, :, cut(j)] = kappa * x
        return carry

    lax.fori_loop(0, chunks, load, 0, unroll=3)
    wrap(state)
    wrap(scaled)


def stage(start_state, final_cotangent, diffusivity, near, far):
    _, _, rows, radial = start_state.shape
    ext = rows + 2 * HALO
    chunks, tiles = ext // SUB, radial // LANES
    f32 = jnp.float32
    vm = pl.BlockSpec(memory_space=pltpu.VMEM)
    outs = (
        (NV, chunks + 2, SUB, radial),
        (NV, chunks, SUB, radial),
        (NV, chunks + 2, SUB, radial),
        (chunks, SUB, radial),
        (chunks, SUB, radial),
    )
    return pl.pallas_call(
        stage_kernel,
        in_specs=[vm] * 5,
        out_specs=[vm] * len(outs),
        out_shape=[jax.ShapeDtypeStruct(shape, f32) for shape in outs],
        scratch_shapes=[
            pltpu.VMEM((NV, tiles, ext, LANES), f32),
            pltpu.VMEM((NV, tiles, ext, LANES), f32),
            pltpu.VMEM((tiles, ext, LANES), f32),
            pltpu.SemaphoreType.DMA((3, tiles)),
        ],
        compiler_params=params(24 * 1024 * 1024),
        name="stage",
    )(start_state, final_cotangent, diffusivity, near, far)


def field_kernel(
    state_0, lam_0, scaled_0, kap, rest, same_0, same_1, other_0, other_1, c_hbm, out,
    c, leaving, states, tanhs, lam, scaled, terms, buf, turned, flip, sems,
):
    chunks, radial = kap.shape[0], kap.shape[2]
    rows = chunks * SUB - 2 * HALO
    tiles = radial // LANES
    own = pl.ds(HALO, rows)

    def cut(j):
        return slice(j * LANES, (j + 1) * LANES)

    c_copy = pltpu.make_async_copy(c_hbm, c, sems.at[NV, 0])
    c_copy.start()
    face_terms(
        (same_0, same_1), (other_0, other_1), c, terms, buf, turned, flip, rows, c_copy.wait
    )
    state = [state_0] + [states.at[n] for n in range(STEPS - 1)]
    spread = [scaled_0] + [scaled.at[n] for n in range(2)]
    lane = iota((SUB, LANES), 1)
    is_first, is_last = lane == 0, lane == LANES - 1

    def neighbours(ref, v, i, j, edge, cache):
        def tile(b):
            if (v, b) not in cache:
                x = ref[v, i + 1, :, cut(b)]
                cache[v, b] = (x, pltpu.roll(x, 1, 1), pltpu.roll(x, LANES - 1, 1))
            return cache[v, b]

        x, r, l = tile(j)
        inn = jnp.where(is_first, tile(j - 1)[1] if j > 0 else 0.0, r)
        outv = jnp.where(is_last, tile(j + 1)[2] if j < tiles - 1 else edge, l)
        return ref[v, i, :, cut(j)] + ref[v, i + 2, :, cut(j)] + inn + outv, x

    def edges(i, n):
        e = terms[pl.ds(i, SUB, stride=chunks), :]
        return [pltpu.roll(e, (2 * LANES - 1 - (n * SUB + v)) % LANES, 1) for v in range(NV)]

    def forward(n):
        def body(i, carry):
            edge = edges(i, n)
            cache = {}
            for j in range(tiles):
                kappa = kap[i, :, cut(j)]
                pairs = [neighbours(state[n], v, i, j, edge[v], cache) for v in range(NV)]
                t = [jnp.tanh(x) for _, x in pairs]
                for v in range(NV):
                    around, x = pairs[v]
                    tanhs[n, v, i, :, cut(j)] = t[v]
                    reaction = sum(c[v, w] * t[w] for w in range(NV))
                    state[n + 1][v, i + 1, :, cut(j)] = (
                        rest[i, :, cut(j)] * x + kappa * around - reaction
                    )
            return carry

        lax.fori_loop(0, chunks, body, 0, unroll=chunks)
        if n + 1 < STEPS - 1:
            wrap(state[n + 1])

    def backward(n, source, target, chosen):
        def body(i, carry):
            edge = edges(i, STEPS - 1 + n)
            cache = {}
            for j in range(tiles):
                kappa = kap[i, :, cut(j)]
                x = [(lam_0 if n == STEPS - 1 else lam)[v, i, :, cut(j)] for v in range(NV)]
                for v in chosen:
                    around, _ = neighbours(spread[source], v, i, j, edge[v], cache)
                    if n < STEPS - 1:
                        t = tanhs[n, v, i, :, cut(j)]
                    else:
                        t = jnp.tanh(state[n][v, i + 1, :, cut(j)])
                    pulled = sum(c[w, v] * x[w] for w in range(NV))
                    new = rest[i, :, cut(j)] * x[v] + around - (1.0 - t * t) * pulled
                    if n > 0:
                        lam[v, i, :, cut(j)] = new
                        spread[target][v, i + 1, :, cut(j)] = kappa * new
                    else:
                        leaving[v, j, pl.ds(i, SUB, stride=chunks), :] = new
            return carry

        lax.fori_loop(0, chunks, body, 0, unroll=chunks)
        if n > 0:
            wrap(spread[target])

    for n in range(STEPS - 1):
        forward(n)
    source = 0
    for n in reversed(range(1, STEPS)):
        target = 2 if source == 1 else 1
        backward(n, source, target, range(NV))
        source = target
    copies = []
    for v in range(NV):
        backward(0, source, None, (v,))
        for j in range(tiles):
            lanes = pl.ds(j * LANES, LANES)
            copies.append(
                pltpu.make_async_copy(
                    leaving.at[v, j, own], out.at[v, 0, :, lanes], sems.at[v, j]
                )
            )
            copies[-1].start()
    for copy in copies:
        copy.wait()


def field(staged, strips, coupling):
    _, chunks, _, radial = staged[1].shape
    ext = chunks * SUB
    rows, tiles, blocks = ext - 2 * HALO, radial // LANES, 2 * strips[0].shape[0]
    vm = pl.BlockSpec(memory_space=pltpu.VMEM)
    hbm = pl.BlockSpec(memory_space=pltpu.HBM)
    f32 = jnp.float32
    return pl.pallas_call(
        field_kernel,
        in_specs=[vm] * 9 + [hbm],
        out_specs=hbm,
        out_shape=jax.ShapeDtypeStruct((NV, 1, rows, radial), f32),
        scratch_shapes=[
            pltpu.SMEM(coupling.shape, f32),
            pltpu.VMEM((NV, tiles, ext, LANES), f32),
            pltpu.VMEM((STEPS - 1, NV, chunks + 2, SUB, radial), f32),
            pltpu.VMEM((STEPS - 1, NV, chunks, SUB, radial), f32),
            pltpu.VMEM((NV, chunks, SUB, radial), f32),
            pltpu.VMEM((2, NV, chunks + 2, SUB, radial), f32),
            pltpu.VMEM((2 * LANES, LANES), f32),
            pltpu.VMEM((2 * STRIP * blocks, LANES), f32),
            pltpu.VMEM(((2 * STEPS - 1) * SUB * blocks, LANES), f32),
            pltpu.VMEM((LANES, 2 * LANES), f32),
            pltpu.SemaphoreType.DMA((NV + 1, tiles)),
        ],
        compiler_params=params(40 * 1024 * 1024),
        name="field",
    )(*staged, *strips, coupling)


def beyond(x):
    size = lax.axis_size("block")
    return lax.ppermute(x, "block", [(i, (i + (1 if i % 2 else -1)) % size) for i in range(size)])


def crossed(x, mask):
    return lax.ppermute(x, "block", [(i, i ^ mask) for i in range(lax.axis_size("block"))])


def swapped(x):
    return lax.ppermute(x, "zone", [(i, i ^ 1) for i in range(lax.axis_size("zone"))])


def gather_pair(strip, first, later):
    x = strip[None]
    bit, size = 1, lax.axis_size("block")
    while 2**bit < size:
        wide = 4 if 2 ** (bit + 1) < size else 2
        pieces = [x] + [crossed(x, k << bit) for k in range(1, wide)]
        *pieces, _ = lax.optimization_barrier((*pieces, first))
        x = jnp.concatenate(pieces, axis=0)
        bit += 2 if wide == 4 else 1
    y = swapped(x)
    y, later = lax.optimization_barrier((y, later))
    return (x, y, crossed(x, 1), crossed(y, 1)), later


def local(
    start_state,
    diffusivity,
    donor_map,
    donor_weight,
    coupling,
    final_cotangent,
    wall_area,
    wall_projection,
    center_ids,
    center_dist,
):
    devices = lax.axis_size("zone") * lax.axis_size("block")
    strip, near, far = pack(
        start_state, final_cotangent, diffusivity, donor_map, donor_weight
    )
    near, far = crossed(near, 1), beyond(far)
    points = wall_gradient(
        start_state, final_cotangent, diffusivity, near, far, coupling, wall_projection,
        wall_area, center_ids, center_dist, devices,
    )
    strips, (near, far) = gather_pair(strip, points, (near, far))
    points = lax.all_to_all(points, ("zone", "block"), 0, 0, tiled=True)

    staged = stage(start_state, final_cotangent, diffusivity, near, far)
    adjoint = field(staged, strips, coupling)
    adjoint, points = lax.optimization_barrier((adjoint, points))
    return adjoint, points.sum(axis=0)


def solution(mesh):
    return jax.shard_map(
        local,
        mesh=mesh,
        in_specs=(
            P(None, "zone", "block", None),
            P("zone", "block", None),
            P(None, "zone", None),
            P(None, "zone", None),
            P(),
            P(None, "zone", "block", None),
            P("zone", "block"),
            P(),
            P("zone", None, "block"),
            P("zone", None, "block"),
        ),
        out_specs=(P(None, "zone", "block", None), P(None, ("zone", "block"))),
        check_vma=False,
    )
```

```python
import functools

import jax
import jax.numpy as jnp
from jax import lax
from jax.experimental import pallas as pl
from jax.experimental.pallas import tpu as pltpu
from jax.sharding import PartitionSpec as P

CP_DEV = 256
LANES = 128
SUB = 8
STEPS = 4
NV = 5
UCOLS = STEPS + 2
LCOLS = STEPS
HALO = SUB
ROW_K = 2 * STEPS
ROW_U = ROW_K + UCOLS
ROW_L = ROW_U + NV * UCOLS
STRIP = ROW_L + NV * LCOLS
EDGE_L = NV * UCOLS
EDGE_K = EDGE_L + NV * LCOLS
EDGE = EDGE_K + UCOLS
TAPS = 6
VMEM_LIMIT = 48 * 1024 * 1024


def params(limit=VMEM_LIMIT):
    return pltpu.CompilerParams(vmem_limit_bytes=limit)


def pack_kernel(
    u_hbm, l_hbm, k_hbm, map_hbm, weight_hbm, strip, near, far,
    u_side, l_side, k_side, u_edge, l_edge, k_edge, dmap, dweight, near_offset, sems,
):
    rows, radial = u_hbm.shape[2], u_hbm.shape[3]
    block = lax.axis_index("block")
    own = pl.ds(pl.multiple_of(block * rows, LANES), rows)
    copies = [
        pltpu.make_async_copy(map_hbm.at[:, 0], dmap, sems.at[0, 0]),
        pltpu.make_async_copy(weight_hbm.at[:, 0, own], dweight, sems.at[0, 1]),
    ]
    lanes = pl.ds(radial - LANES, LANES)
    copies += [
        pltpu.make_async_copy(u_hbm.at[:, 0, :, lanes], u_side, sems.at[1, 0]),
        pltpu.make_async_copy(l_hbm.at[:, 0, :, lanes], l_side, sems.at[2, 0]),
        pltpu.make_async_copy(k_hbm.at[0, :, lanes], k_side, sems.at[3, 0]),
    ]
    lower = block % 2 == 0
    top = jnp.where(lower, rows - SUB, 0)
    for i, start in enumerate((top, rows - SUB - top)):
        some = pl.ds(pl.multiple_of(start, SUB), SUB)
        copies += [
            pltpu.make_async_copy(u_hbm.at[:, 0, some], u_edge.at[i], sems.at[4, i]),
            pltpu.make_async_copy(l_hbm.at[:, 0, some], l_edge.at[i], sems.at[5, i]),
            pltpu.make_async_copy(k_hbm.at[0, some], k_edge.at[i], sems.at[6, i]),
        ]
    for copy in copies:
        copy.start()
    for copy in copies[:2]:
        copy.wait()
    size = dmap.shape[1]
    delta = dmap[...] - iota(dmap.shape, 1)
    delta = jnp.where(delta < 0, delta + size, delta)
    ahead = delta - delta[:, 0:1] + STEPS
    ahead = jnp.where(ahead < 0, ahead + size, ahead)
    ahead = jnp.where(ahead >= size, ahead - size, ahead).astype(jnp.float32)
    least = jnp.min(ahead, axis=1, keepdims=True)
    offset = delta[:, 0:1].astype(jnp.float32) - float(STEPS) + least
    offset = jnp.where(offset < 0.0, offset + float(size), offset)
    offset = jnp.where(offset >= float(size), offset - float(size), offset)
    near_offset[...] = ahead - least
    strip[0:STEPS, :] = near_offset[:, own]
    which = iota((STEPS, rows), 1) == iota((STEPS, rows), 0)
    offsets = jnp.sum(jnp.where(which, offset, 0.0), axis=0, keepdims=True)
    strip[STEPS : 2 * STEPS, :] = dweight[...]
    for copy in copies[2:5]:
        copy.wait()
    strip[ROW_K : ROW_K + 1, :] = offsets
    strip[ROW_K + 1 : ROW_K + UCOLS, :] = k_side[...].T[LANES - UCOLS + 1 :]
    for v in range(NV):
        a, b = ROW_U + v * UCOLS, ROW_L + v * LCOLS
        strip[a : a + UCOLS, :] = u_side[v].T[LANES - UCOLS :]
        strip[b : b + LCOLS, :] = l_side[v].T[LANES - LCOLS :]
    for copy in copies[5:]:
        copy.wait()
    for i, ref in enumerate((near, far)):
        last = lower if i == 0 else jnp.logical_not(lower)

        def ends(x, count):
            return jnp.where(last, x[SUB - count :], x[:count])

        for v in range(NV):
            ref[v * UCOLS : (v + 1) * UCOLS, :] = ends(u_edge[i, v], UCOLS)
            ref[EDGE_L + v * LCOLS : EDGE_L + (v + 1) * LCOLS, :] = ends(l_edge[i, v], LCOLS)
        ref[EDGE_K:EDGE, :] = ends(k_edge[i], UCOLS)


def pack(start_state, final_cotangent, diffusivity, donor_map, donor_weight):
    _, _, rows, radial = start_state.shape
    f32 = jnp.float32
    outs = ((STRIP, rows), (EDGE, radial), (EDGE, radial))
    return pl.pallas_call(
        pack_kernel,
        in_specs=[pl.BlockSpec(memory_space=pltpu.HBM)] * 5,
        out_specs=[pl.BlockSpec(memory_space=pltpu.VMEM)] * 3,
        out_shape=[jax.ShapeDtypeStruct(s, f32) for s in outs],
        scratch_shapes=[
            pltpu.VMEM((NV, rows, LANES), f32),
            pltpu.VMEM((NV, rows, LANES), f32),
            pltpu.VMEM((rows, LANES), f32),
            pltpu.VMEM((2, NV, SUB, radial), f32),
            pltpu.VMEM((2, NV, SUB, radial), f32),
            pltpu.VMEM((2, SUB, radial), f32),
            pltpu.VMEM((STEPS, donor_map.shape[2]), jnp.int32),
            pltpu.VMEM((STEPS, rows), f32),
            pltpu.VMEM((STEPS, donor_map.shape[2]), f32),
            pltpu.SemaphoreType.DMA((7, 2)),
        ],
        compiler_params=params(),
        name="pack",
    )(
        *(
            pltpu.with_memory_space_constraint(x, pltpu.HBM)
            for x in (start_state, final_cotangent, diffusivity, donor_map, donor_weight)
        )
    )


def iota(shape, axis):
    return lax.broadcasted_iota(jnp.int32, shape, axis)


def left(x, by=1):
    return pltpu.roll(x, x.shape[-1] - by, x.ndim - 1)


def right(x, by=1):
    return pltpu.roll(x, by, x.ndim - 1)


def stencil(x):
    inn = jnp.where(iota(x.shape, 0) == 0, 0.0, pltpu.roll(x, 1, 0))
    return left(x) + right(x) + pltpu.roll(x, SUB - 1, 0) + inn - 4.0 * x


def strip_forward(u, t, kappa, c):
    new = []
    for v in range(NV):
        reaction = sum(c[v, w] * t[w] for w in range(NV))
        new.append(u[v] + kappa * stencil(u[v]) - reaction)
    return new


def strip_backward(lam, t, kappa, c):
    new = []
    for v in range(NV):
        pulled = sum(c[w, v] * lam[w] for w in range(NV))
        new.append(lam[v] + stencil(kappa * lam[v]) - (1.0 - t[v] * t[v]) * pulled)
    return new


def wall_kernel(
    u_own, l_own, k_own, near, far, c_ref, proj_ref, area, ids, dist, out, *, devices
):
    rows, nodes = u_own.shape[2], area.shape[1]
    c = {(v, w): c_ref[v : v + 1, w : w + 1] for v in range(NV) for w in range(NV)}
    proj = {(i, v): proj_ref[i : i + 1, v : v + 1] for i in range(3) for v in range(NV)}
    lower = lax.axis_index("block") % 2 == 0
    x, y = near[:, 0:LANES], far[:, 0:LANES]
    gap = jnp.zeros((LANES - 2 * EDGE, LANES), jnp.float32)
    halos = jnp.concatenate([jnp.where(lower, y, x), jnp.where(lower, x, y), gap], axis=0).T[:SUB]
    lane = iota((SUB, LANES), 1)

    def first(own, edge, cols):
        after = pltpu.roll(halos, (LANES - EDGE - edge) % LANES, 1)
        before = pltpu.roll(halos, (LANES - cols - edge) % LANES, 1)
        beside = jnp.where(lane < cols, after, jnp.where(lane >= LANES - cols, before, 0.0))
        return jnp.concatenate([own[:, :LANES].T[:SUB], beside], axis=1)

    kappa = first(k_own.at[0], EDGE_K, UCOLS)
    u = [first(u_own.at[v, 0], v * UCOLS, UCOLS) for v in range(NV)]
    lam = [first(l_own.at[v, 0], EDGE_L + v * LCOLS, LCOLS) for v in range(NV)]
    history = []
    for n in range(STEPS):
        t = [jnp.tanh(x) for x in u]
        history.append((u, t))
        if n < STEPS - 1:
            u = strip_forward(u, t, kappa, c)
    h = [0.0] * NV
    for n in reversed(range(STEPS)):
        u, t = history[n]
        h = [h[v] + (lam[v] * u[v])[0:1, :rows] for v in range(NV)]
        if n > 0:
            lam = strip_backward(lam, t, kappa, c)
    per_row = nodes // rows
    groups = CP_DEV // LANES
    components = [sum(proj[i, v] * h[v] for v in range(NV)) for i in range(3)]
    components += [jnp.zeros((SUB // groups - 3, rows), jnp.float32)]
    s_rows = components * groups
    spread = (iota((rows, nodes), 1) // per_row == iota((rows, nodes), 0)).astype(jnp.float32)
    s = jnp.dot(
        jnp.concatenate(s_rows, axis=0), spread,
        precision=lax.Precision.HIGHEST, preferred_element_type=jnp.float32,
    )
    s = s * area[...]
    d = dist[0]
    q = 1.0 - d
    q = q * q
    phi = q * q * (4.0 * d + 1.0)
    key = ids[0]
    major, minor = key // LANES, key % LANES
    shape = (devices, SUB, nodes)
    target = iota(shape, 0) * groups + iota(shape, 1) // (SUB // groups)
    total = jnp.zeros((devices * SUB, LANES), jnp.float32)
    bf = jnp.bfloat16
    for k in range(d.shape[0]):
        lo = (iota((LANES, nodes), 0) == minor[k : k + 1]).astype(bf)
        hit = target == major[k : k + 1][None]
        w = s * phi[k : k + 1]
        for piece in range(2):
            part = w.astype(bf).astype(jnp.float32)
            w = w - part
            a = jnp.where(hit, part[None], 0.0).reshape(devices * SUB, nodes).astype(bf)
            total += lax.dot_general(
                a, lo, (((1,), (1,)), ((), ())), preferred_element_type=jnp.float32
            )
    total = total.reshape(devices, SUB, LANES)
    for g in range(groups):
        start = g * (SUB // groups)
        out[:, :, g * LANES : (g + 1) * LANES] = total[:, start : start + 3]


def wall_gradient(u, lam, kappa, near, far, coupling, proj, area, ids, dist, devices):
    vm = pl.BlockSpec(memory_space=pltpu.VMEM)
    return pl.pallas_call(
        functools.partial(wall_kernel, devices=devices),
        in_specs=[vm] * 10,
        out_specs=vm,
        out_shape=jax.ShapeDtypeStruct((devices, 3, CP_DEV), jnp.float32),
        compiler_params=params(),
        name="wall_gradient",
    )(u, lam, kappa, near, far, coupling, proj, area, ids, dist)


def face_terms(same, other, c, out, buf, turned, flip, rows, ready):
    block = lax.axis_index("block")
    blocks = 2 * same[0].shape[0]
    shape = (blocks, LANES)
    for m in range(blocks // 2):
        at = block ^ (2 * m)
        for q in range(2):
            start = q * STRIP * blocks
            buf[pl.ds(start + at, STRIP, stride=blocks), :] = same[q][m]
            buf[pl.ds(start + (at ^ 1), STRIP, stride=blocks), :] = other[q][m]

    def load(q, row):
        return buf[pl.ds((q * STRIP + row) * blocks, blocks), :]

    lane = iota(shape, 1)

    def later(x, by=1):
        y = jnp.where(lane >= by, x, pltpu.roll(x, blocks - 1, 0))
        return pltpu.roll(y, LANES - by, 1)

    def earlier(x, by=1):
        y = jnp.where(lane < LANES - by, x, pltpu.roll(x, 1, 0))
        return pltpu.roll(y, by, 1)

    far, taps = {}, {}
    for q in range(2):
        for n in range(STEPS):
            t = load(q, ROW_K)[0:1, n : n + 1].astype(jnp.int32)[0, 0]
            far[q, n] = (t // LANES, t % LANES)
            e = load(q, n)
            share = load(q, STEPS + n)
            taps[q, n] = [
                jnp.where(e == float(i), share, 0.0)
                + jnp.where(e == float(i - 1), 1.0 - share, 0.0)
                for i in range(TAPS)
            ]

    def shifts(q, n):
        whole, rest = far[q, n]
        return whole, [
            (jnp.where(rest + i < LANES, rest + i, rest + i - LANES), lane >= rest + i,
             lane >= rest + i - LANES)
            for i in range(TAPS)
        ]

    def ghost(q, n, faces):
        whole, moves = shifts(q, n)
        result = []
        for f in faces:
            near = [pltpu.roll(f, (2 * blocks - whole - k) % blocks, 0) for k in range(3)]
            acc = 0.0
            for i, (by, here, next_one) in enumerate(moves):
                y = jnp.where(here, near[0], jnp.where(next_one, near[1], near[2]))
                acc = acc + taps[q, n][i] * pltpu.roll(y, (LANES - by) % LANES, 1)
            result.append(acc)
        return result

    def back(q, n, faces):
        whole, moves = shifts(q, n)
        result = []
        for f in faces:
            parts = [0.0, 0.0, 0.0]
            for i, (by, here, next_one) in enumerate(moves):
                y = pltpu.roll(taps[q, n][i] * f, by, 1)
                parts[0] = parts[0] + jnp.where(here, y, 0.0)
                parts[1] = parts[1] + jnp.where(here, 0.0, jnp.where(next_one, y, 0.0))
                parts[2] = parts[2] + jnp.where(next_one, 0.0, y)
            result.append(
                sum(pltpu.roll(parts[k], (whole + k) % blocks, 0) for k in range(3))
            )
        return result

    def emit(index, g):
        for v in range(NV):
            turned[pl.ds((index * SUB + v) * blocks, blocks), :] = g[v]

    last = UCOLS - 1
    kappa = [[load(q, ROW_K + k) for k in range(UCOLS)] for q in range(2)]
    u = [
        [{k: load(q, ROW_U + v * UCOLS + k) for k in range(UCOLS)} for v in range(NV)]
        for q in range(2)
    ]
    gap = UCOLS - LCOLS
    lam = [
        [{k: load(q, ROW_L + v * LCOLS + k - gap) for k in range(gap, UCOLS)} for v in range(NV)]
        for q in range(2)
    ]
    history = {}
    ready()
    for n in range(STEPS):
        first = n + 1 if n < STEPS - 1 else STEPS - 1
        for q in range(2):
            history[n, q] = [
                {k: jnp.tanh(u[q][v][k]) for k in range(first, UCOLS)} for v in range(NV)
            ]
        if n == STEPS - 1:
            break
        g = [ghost(q, n, [u[1 - q][v][last] for v in range(NV)]) for q in range(2)]
        emit(n, g[0])
        new = []
        for q in range(2):
            side = []
            for v in range(NV):
                cols = {}
                for k in range(n + 1, UCOLS):
                    x = u[q][v][k]
                    outer = u[q][v][k + 1] if k < last else g[q][v]
                    lap = later(x) + earlier(x) + u[q][v][k - 1] + outer - 4.0 * x
                    reaction = sum(c[v, w] * history[n, q][w][k] for w in range(NV))
                    cols[k] = x + kappa[q][k] * lap - reaction
                side.append(cols)
            new.append(side)
        u = new
    for n in reversed(range(STEPS)):
        s = [
            [{k: kappa[q][k] * x for k, x in lam[q][v].items()} for v in range(NV)]
            for q in range(2)
        ]
        sides = (0, 1) if n > 1 else (1,) if n == 1 else ()
        g = {
            q: back(1 - q, n, [s[1 - q][v][last] for v in range(NV)]) for q in {0, *sides}
        }
        emit(STEPS - 1 + n, g[0])
        new = [None, None]
        for q in sides:
            side = []
            for v in range(NV):
                cols = {}
                for k in range(UCOLS - n, UCOLS):
                    x = lam[q][v][k]
                    y = s[q][v][k]
                    outer = s[q][v][k + 1] if k < last else g[q][v]
                    lap = later(y) + earlier(y) + s[q][v][k - 1] + outer - 4.0 * y
                    pulled = sum(c[w, v] * lam[q][w][k] for w in range(NV))
                    t = history[n, q][v][k]
                    cols[k] = x + lap - (1.0 - t * t) * pulled
                side.append(cols)
            new[q] = side
        if n == 1:
            new[0] = [{last: jnp.zeros(shape, jnp.float32)} for v in range(NV)]
        lam = new

    count = (2 * STEPS - 1) * SUB
    flip[...] = jnp.zeros_like(flip)
    around = [
        turned[pl.ds(lax.rem(block + shift + blocks, blocks), count, stride=blocks), :]
        for shift in (-1, 0, 1)
    ]
    wide = jnp.concatenate(around, axis=1)
    wide = pltpu.roll(wide, wide.shape[1] - (LANES - HALO), 1)
    flip[0:count, :] = wide[:, : 2 * LANES]
    for j in range(2):
        out[j * LANES : (j + 1) * LANES, :] = flip[:, j * LANES : (j + 1) * LANES].T


def wrap(ref):
    chunks = ref.shape[1] - 2
    for v in range(NV):
        ref[v, 0] = pltpu.roll(ref[v, chunks], 1, 0)
        ref[v, chunks + 1] = pltpu.roll(ref[v, 1], SUB - 1, 0)


def stage_kernel(
    u_own, l_own, k_own, near, far, state, lam, scaled, kap, rest, ext_u, ext_l, ext_k, sems
):
    rows, radial = u_own.shape[2], u_own.shape[3]
    chunks = kap.shape[0]
    tiles = radial // LANES
    own = pl.ds(HALO, rows)

    def cut(j):
        return slice(j * LANES, (j + 1) * LANES)

    copies = []
    for j in range(tiles):
        lanes = pl.ds(j * LANES, LANES)
        copies += [
            pltpu.make_async_copy(u_own.at[:, 0, :, lanes], ext_u.at[:, j, own], sems.at[0, j]),
            pltpu.make_async_copy(l_own.at[:, 0, :, lanes], ext_l.at[:, j, own], sems.at[1, j]),
            pltpu.make_async_copy(k_own.at[0, :, lanes], ext_k.at[j, own], sems.at[2, j]),
        ]
    for copy in copies:
        copy.start()
    lower = lax.axis_index("block") % 2 == 0

    def halo(a, b, cols):
        x, y = near[a:b, cols], far[a:b, cols]
        return jnp.where(lower, y, x), jnp.where(lower, x, y)

    def put(ref, where, pair, count):
        gap = jnp.zeros((HALO - count, LANES), jnp.float32)
        ref[(*where, pl.ds(0, HALO))] = jnp.concatenate([gap, pair[0]], axis=0)
        ref[(*where, pl.ds(HALO + rows, HALO))] = jnp.concatenate([pair[1], gap], axis=0)

    for j in range(tiles):
        put(ext_k, (j,), halo(EDGE_K, EDGE, cut(j)), UCOLS)
        for v in range(NV):
            put(ext_u, (v, j), halo(v * UCOLS, (v + 1) * UCOLS, cut(j)), UCOLS)
            at = EDGE_L + v * LCOLS
            put(ext_l, (v, j), halo(at, at + LCOLS, cut(j)), LCOLS)
    for copy in copies:
        copy.wait()

    def load(i, carry):
        at = pl.ds(i, SUB, stride=chunks)
        for j in range(tiles):
            kappa = ext_k[j, at, :]
            kap[i, :, cut(j)] = kappa
            rest[i, :, cut(j)] = 1.0 - 4.0 * kappa
            for v in range(NV):
                state[v, i + 1, :, cut(j)] = ext_u[v, j, at, :]
                x = ext_l[v, j, at, :]
                lam[v, i, :, cut(j)] = x
                scaled[v, i + 1, :, cut(j)] = kappa * x
        return carry

    lax.fori_loop(0, chunks, load, 0, unroll=3)
    wrap(state)
    wrap(scaled)


def stage(start_state, final_cotangent, diffusivity, near, far):
    _, _, rows, radial = start_state.shape
    ext = rows + 2 * HALO
    chunks, tiles = ext // SUB, radial // LANES
    f32 = jnp.float32
    vm = pl.BlockSpec(memory_space=pltpu.VMEM)
    outs = (
        (NV, chunks + 2, SUB, radial),
        (NV, chunks, SUB, radial),
        (NV, chunks + 2, SUB, radial),
        (chunks, SUB, radial),
        (chunks, SUB, radial),
    )
    return pl.pallas_call(
        stage_kernel,
        in_specs=[vm] * 5,
        out_specs=[vm] * len(outs),
        out_shape=[jax.ShapeDtypeStruct(shape, f32) for shape in outs],
        scratch_shapes=[
            pltpu.VMEM((NV, tiles, ext, LANES), f32),
            pltpu.VMEM((NV, tiles, ext, LANES), f32),
            pltpu.VMEM((tiles, ext, LANES), f32),
            pltpu.SemaphoreType.DMA((3, tiles)),
        ],
        compiler_params=params(24 * 1024 * 1024),
        name="stage",
    )(start_state, final_cotangent, diffusivity, near, far)


def field_kernel(
    state_0, lam_0, scaled_0, kap, rest, same_0, same_1, other_0, other_1, c_hbm, out,
    c, leaving, states, tanhs, lam, scaled, terms, buf, turned, flip, sems,
):
    chunks, radial = kap.shape[0], kap.shape[2]
    rows = chunks * SUB - 2 * HALO
    tiles = radial // LANES
    own = pl.ds(HALO, rows)

    def cut(j):
        return slice(j * LANES, (j + 1) * LANES)

    c_copy = pltpu.make_async_copy(c_hbm, c, sems.at[NV, 0])
    c_copy.start()
    face_terms(
        (same_0, same_1), (other_0, other_1), c, terms, buf, turned, flip, rows, c_copy.wait
    )
    state = [state_0] + [states.at[n] for n in range(STEPS - 2)]
    spread = [scaled_0] + [scaled.at[n] for n in range(2)]
    lane = iota((SUB, LANES), 1)
    is_first, is_last = lane == 0, lane == LANES - 1

    def neighbours(ref, v, i, j, edge, cache):
        def tile(b):
            if (v, b) not in cache:
                x = ref[v, i + 1, :, cut(b)]
                cache[v, b] = (x, pltpu.roll(x, 1, 1), pltpu.roll(x, LANES - 1, 1))
            return cache[v, b]

        x, r, l = tile(j)
        inn = jnp.where(is_first, tile(j - 1)[1] if j > 0 else 0.0, r)
        outv = jnp.where(is_last, tile(j + 1)[2] if j < tiles - 1 else edge, l)
        return ref[v, i, :, cut(j)] + ref[v, i + 2, :, cut(j)] + inn + outv, x

    def edges(i, n):
        e = terms[pl.ds(i, SUB, stride=chunks), :]
        return [pltpu.roll(e, (2 * LANES - 1 - (n * SUB + v)) % LANES, 1) for v in range(NV)]

    def pull(v, i, j, x, t, around):
        pulled = sum(c[w, v] * x[w] for w in range(NV))
        return rest[i, :, cut(j)] * x[v] + around - (1.0 - t * t) * pulled

    def forward(n):
        joined = n == STEPS - 2

        def body(i, carry):
            edge = edges(i, n)
            cache, back_cache = {}, {}
            if joined:
                back_edge = edges(i, 2 * STEPS - 2)
            for j in range(tiles):
                kappa = kap[i, :, cut(j)]
                pairs = [neighbours(state[n], v, i, j, edge[v], cache) for v in range(NV)]
                t = [jnp.tanh(x) for _, x in pairs]
                if joined:
                    lams = [lam_0[v, i, :, cut(j)] for v in range(NV)]
                for v in range(NV):
                    around, x = pairs[v]
                    tanhs[n, v, i, :, cut(j)] = t[v]
                    reaction = sum(c[v, w] * t[w] for w in range(NV))
                    new = rest[i, :, cut(j)] * x + kappa * around - reaction
                    if joined:
                        around, _ = neighbours(scaled_0, v, i, j, back_edge[v], back_cache)
                        y = pull(v, i, j, lams, jnp.tanh(new), around)
                        lam[v, i, :, cut(j)] = y
                        spread[1][v, i + 1, :, cut(j)] = kappa * y
                    else:
                        state[n + 1][v, i + 1, :, cut(j)] = new
            return carry

        lax.fori_loop(0, chunks, body, 0, unroll=chunks)
        wrap(spread[1] if joined else state[n + 1])

    def backward(n, source, target, chosen):
        def body(i, carry):
            edge = edges(i, STEPS - 1 + n)
            cache = {}
            for j in range(tiles):
                kappa = kap[i, :, cut(j)]
                x = [lam[v, i, :, cut(j)] for v in range(NV)]
                for v in chosen:
                    around, _ = neighbours(spread[source], v, i, j, edge[v], cache)
                    new = pull(v, i, j, x, tanhs[n, v, i, :, cut(j)], around)
                    if n > 0:
                        lam[v, i, :, cut(j)] = new
                        spread[target][v, i + 1, :, cut(j)] = kappa * new
                    else:
                        leaving[v, j, pl.ds(i, SUB, stride=chunks), :] = new
            return carry

        lax.fori_loop(0, chunks, body, 0, unroll=chunks)
        if n > 0:
            wrap(spread[target])

    for n in range(STEPS - 1):
        forward(n)
    source = 1
    for n in reversed(range(1, STEPS - 1)):
        target = 2 if source == 1 else 1
        backward(n, source, target, range(NV))
        source = target
    copies = []
    for v in range(NV):
        backward(0, source, None, (v,))
        for j in range(tiles):
            lanes = pl.ds(j * LANES, LANES)
            copies.append(
                pltpu.make_async_copy(
                    leaving.at[v, j, own], out.at[v, 0, :, lanes], sems.at[v, j]
                )
            )
            copies[-1].start()
    for copy in copies:
        copy.wait()


def field(staged, strips, coupling):
    _, chunks, _, radial = staged[1].shape
    ext = chunks * SUB
    rows, tiles, blocks = ext - 2 * HALO, radial // LANES, 2 * strips[0].shape[0]
    vm = pl.BlockSpec(memory_space=pltpu.VMEM)
    hbm = pl.BlockSpec(memory_space=pltpu.HBM)
    f32 = jnp.float32
    return pl.pallas_call(
        field_kernel,
        in_specs=[vm] * 9 + [hbm],
        out_specs=hbm,
        out_shape=jax.ShapeDtypeStruct((NV, 1, rows, radial), f32),
        scratch_shapes=[
            pltpu.SMEM(coupling.shape, f32),
            pltpu.VMEM((NV, tiles, ext, LANES), f32),
            pltpu.VMEM((STEPS - 2, NV, chunks + 2, SUB, radial), f32),
            pltpu.VMEM((STEPS - 1, NV, chunks, SUB, radial), f32),
            pltpu.VMEM((NV, chunks, SUB, radial), f32),
            pltpu.VMEM((2, NV, chunks + 2, SUB, radial), f32),
            pltpu.VMEM((2 * LANES, LANES), f32),
            pltpu.VMEM((2 * STRIP * blocks, LANES), f32),
            pltpu.VMEM(((2 * STEPS - 1) * SUB * blocks, LANES), f32),
            pltpu.VMEM((LANES, 2 * LANES), f32),
            pltpu.SemaphoreType.DMA((NV + 1, tiles)),
        ],
        compiler_params=params(40 * 1024 * 1024),
        name="field",
    )(*staged, *strips, coupling)


def beyond(x):
    size = lax.axis_size("block")
    return lax.ppermute(x, "block", [(i, (i + (1 if i % 2 else -1)) % size) for i in range(size)])


def crossed(x, mask):
    return lax.ppermute(x, "block", [(i, i ^ mask) for i in range(lax.axis_size("block"))])


def swapped(x):
    return lax.ppermute(x, "zone", [(i, i ^ 1) for i in range(lax.axis_size("zone"))])


def gather_pair(strip, first, later):
    x = strip[None]
    bit, size = 1, lax.axis_size("block")
    while 2**bit < size:
        wide = 4 if 2 ** (bit + 1) < size else 2
        pieces = [x] + [crossed(x, k << bit) for k in range(1, wide)]
        *pieces, _ = lax.optimization_barrier((*pieces, first))
        x = jnp.concatenate(pieces, axis=0)
        bit += 2 if wide == 4 else 1
    y = swapped(x)
    y, later = lax.optimization_barrier((y, later))
    return (x, y, crossed(x, 1), crossed(y, 1)), later


def local(
    start_state,
    diffusivity,
    donor_map,
    donor_weight,
    coupling,
    final_cotangent,
    wall_area,
    wall_projection,
    center_ids,
    center_dist,
):
    devices = lax.axis_size("zone") * lax.axis_size("block")
    strip, near, far = pack(
        start_state, final_cotangent, diffusivity, donor_map, donor_weight
    )
    near, far = crossed(near, 1), beyond(far)
    points = wall_gradient(
        start_state, final_cotangent, diffusivity, near, far, coupling, wall_projection,
        wall_area, center_ids, center_dist, devices,
    )
    strips, (near, far) = gather_pair(strip, points, (near, far))
    points = lax.all_to_all(points, ("zone", "block"), 0, 0, tiled=True)

    staged = stage(start_state, final_cotangent, diffusivity, near, far)
    adjoint = field(staged, strips, coupling)
    adjoint, points = lax.optimization_barrier((adjoint, points))
    return adjoint, points.sum(axis=0)


def solution(mesh):
    return jax.shard_map(
        local,
        mesh=mesh,
        in_specs=(
            P(None, "zone", "block", None),
            P("zone", "block", None),
            P(None, "zone", None),
            P(None, "zone", None),
            P(),
            P(None, "zone", "block", None),
            P("zone", "block"),
            P(),
            P("zone", None, "block"),
            P("zone", None, "block"),
        ),
        out_specs=(P(None, "zone", "block", None), P(None, ("zone", "block"))),
        check_vma=False,
    )
```
